256 devices in a mesh: row: 16 (over z, core), col: 16 (over y, x).
Axes of the slice: x: 4, y: 4, z: 8, core: 2. Of those that a mesh axis runs over, the one named last changes fastest.
Arguments:
- old_factor: float32 [2, 4096, 2, 4096], P(None, 'row', None, 'col'), may hold values from -32 to 32
- panel_block: float32 [2, 4096, 1024], P(None, 'row'), may hold values from -4 to 4, as said below
Outputs:
- panel_factor: float32 [2, 4096, 1024], P(None, 'row', 'col')
The draws below stay inside these ranges and needn't reach their ends.
Inputs may be any that keep to these rules, and one draw needn't show every extreme that they name: `panel_block`: the two diagonal blocks of 512 x 512 of entries (rows and columns [s * 512, (s + 1) * 512)) are symmetric up to rounding; for s = 0 and 1 the block schur_s[s * 512:(s + 1) * 512, :] is symmetric up to rounding and has no eigenvalue under 0.05.
All inputs are finite; a program needn't handle non-finite values.
Results may differ from the reference program's by a relative error of at most 0.0003.
Values sent between devices are 32-bit elements; how exact they have to be, the bound alone decides.
A program may use at most 64 MiB of HBM per device.

```python
import math
import jax
import jax.numpy as jnp
from jax import lax

TILE = 256
PW = 512
RT_DEV = 2
KT_DEV = 2
WROWS = 8192
KOLD = 8192
N_ROW = 16
N_COL = 16


ridge = 0.1


spread = 2.0


def earlier_columns(key, far_gain):
    key = jax.random.fold_in(key, 5)
    normal_key = jax.random.fold_in(key, 11)
    normal_draw = jax.random.truncated_normal(normal_key, -2.96, 2.96, (WROWS, KOLD), jnp.float32)
    values = normal_draw
    band_scale = math.sqrt(0.01 / math.sqrt(PW * KOLD))
    far_scale = far_gain / (band_scale * math.sqrt(KOLD))
    position = jnp.arange(WROWS, dtype=jnp.int32)
    row_scale = jnp.where(position < 2 * PW, band_scale, far_scale)
    return values * row_scale[:, None]


def draw_old_factor(key, part):
    earlier = earlier_columns(key, 1.0)
    return earlier.reshape(RT_DEV, TILE * N_ROW, KT_DEV, TILE * N_COL)


def draw_panel_block(key, part):
    own_key = jax.random.fold_in(key, 7)
    earlier = earlier_columns(key, 1.0)
    centres = jax.random.normal(own_key, (WROWS, 8), jnp.float32)
    band_span = 2 * PW
    square = jnp.zeros((WROWS, band_span), jnp.float32)
    for coordinate in range(8):
        difference = centres[:, coordinate][:, None] - centres[:band_span, coordinate][None, :]
        square = square + difference * difference
    kernel = jnp.exp(square * (-0.5 / (spread * spread)))
    position = jnp.arange(WROWS, dtype=jnp.int32)
    column_index = jnp.arange(band_span, dtype=jnp.int32)
    kernel = kernel + jnp.where(position[:, None] == column_index[None, :], ridge, 0.0)
    entries = kernel + jnp.dot(earlier, earlier[:band_span].T, precision=lax.Precision.HIGHEST, preferred_element_type=jnp.float32)
    entries = jnp.where(position[:, None] < band_span, entries, jnp.clip(entries, -4.0, 4.0))
    return entries.reshape(RT_DEV, TILE * N_ROW, band_span)


def setup_inputs(seed: int = 0) -> dict:
    key_list = jax.random.split(jax.random.key(seed), 3)
    old_factor = draw_old_factor(jax.random.fold_in(key_list[2], 71), 0)
    panel_block = draw_panel_block(jax.random.fold_in(key_list[2], 71), 0)
    return dict(old_factor=old_factor, panel_block=panel_block)


def reference(old_factor, panel_block):
    earlier_block = old_factor.reshape(WROWS, KOLD)
    entries = panel_block.reshape(WROWS, 2 * PW)
    global_row = jnp.arange(WROWS, dtype=jnp.int32)
    columns = jnp.arange(PW, dtype=jnp.int32)
    finished = []
    for section_index in range(2):
        band_start = section_index * PW
        schur_block = entries[:, band_start:band_start + PW] - jnp.dot(earlier_block.astype(jnp.float32), earlier_block[band_start:band_start + PW].T.astype(jnp.float32), precision=lax.Precision.HIGHEST, preferred_element_type=jnp.float32)
        for earlier_part in finished:
            schur_block = schur_block - jnp.dot(earlier_part.astype(jnp.float32), earlier_part[band_start:band_start + PW].T.astype(jnp.float32), precision=lax.Precision.HIGHEST, preferred_element_type=jnp.float32)
        cholesky_lower = jnp.linalg.cholesky(schur_block[band_start:band_start + PW])
        solved = jax.scipy.linalg.solve_triangular(cholesky_lower, schur_block.T, lower=True).T
        keep_mask = columns[None, :] <= (global_row - band_start)[:, None]
        finished.append(jnp.where(keep_mask, solved, jnp.zeros_like(solved)))
    joined = jnp.concatenate(finished, axis=1)
    return joined.reshape(RT_DEV, TILE * N_ROW, 2 * PW)
```

```python
import jax
import jax.numpy as jnp
from jax import lax
from jax.experimental import pallas as pl
from jax.experimental.pallas import tpu as pltpu
from jax.sharding import PartitionSpec as P

F32 = jnp.float32
MESH = pl.DeviceIdType.MESH
BLK = 128
NB = 8
SUPER = 2


def lane(x, k):
    return jnp.broadcast_to(x[:, k : k + 1], (8, BLK))


def sub(x, k):
    return jnp.broadcast_to(x[k : k + 1, :], (8, BLK))


def dot_tn(a, b):
    return lax.dot_general(
        a, b, (((0,), (0,)), ((), ())), precision=lax.Precision.HIGHEST, preferred_element_type=F32
    )


def dot_nt(a, b):
    return lax.dot_general(
        a, b, (((1,), (1,)), ((), ())), precision=lax.Precision.HIGHEST, preferred_element_type=F32
    )


def factor_inverse(read, write):
    idx = lax.broadcasted_iota(jnp.int32, (8, BLK), 0)
    col = lax.broadcasted_iota(jnp.int32, (8, BLK), 1)
    groups = BLK // 8
    m = [read(i) for i in range(groups)]
    w = [jnp.where(col == idx + 8 * i, 1.0, 0.0).astype(F32) for i in range(groups)]
    u = [None] * groups
    uw = [None] * groups
    for g in range(groups):
        sb = g // SUPER
        near = list(range(g + 1, min(groups, SUPER * (sb + 2))))
        t, v = m[g], w[g]
        piv = [lane(t, 8 * g + k) for k in range(8)]
        low = {i: [lane(m[i], 8 * g + k) for k in range(8)] for i in near}
        rows, rows_w, mult = [], [], {i: [] for i in near}
        for k in range(8):
            scale = lax.rsqrt(sub(piv[k], k))
            mk = jnp.where(idx > k, piv[k] * scale, 0.0)
            rk, rwk = sub(t, k) * scale, sub(v, k) * scale
            rows.append(rk)
            rows_w.append(rwk)
            if k < 7:
                t, v = t - mk * rk, v - mk * rwk
            for i in near:
                mult[i].append(low[i][k] * scale)
            for n in range(k + 1, 8):
                q = sub(piv[n], k) * scale
                piv[n] = piv[n] - mk * q
                for i in near:
                    low[i][n] = low[i][n] - mult[i][k] * q
        ug, uwg = rows[0], rows_w[0]
        for k in range(1, 8):
            ug, uwg = jnp.where(idx == k, rows[k], ug), jnp.where(idx == k, rows_w[k], uwg)
        u[g], uw[g] = ug, uwg
        write(g, uwg)
        for i in near:
            a, b = m[i], w[i]
            for k in range(8):
                a, b = a - mult[i][k] * rows[k], b - mult[i][k] * rows_w[k]
            m[i], w[i] = a, b
        first = SUPER * (sb + 2)
        if g % SUPER == SUPER - 1 and first < groups:
            us = jnp.concatenate(u[SUPER * sb : g + 1], axis=0)
            ws = jnp.concatenate(uw[SUPER * sb : g + 1], axis=0)
            eu, ew = dot_tn(us, us), dot_tn(us, ws)
            for i in range(first, groups):
                m[i], w[i] = m[i] - eu[8 * i : 8 * i + 8], w[i] - ew[8 * i : 8 * i + 8]


def kernel(
    a_ref, e_hbm, out_ref,
    band, part, rs1, rs2, drs, dt, cm, winv, stage, outv, ebuf,
    e_sem, ring_s, ring_r, back_s, sib_s, sib_r,
    d_s, d_r, z_s, z_r, g1_s, g1_r, g2_s, g2_r, gs_s, gs_r,
    r1_s, r1_r, r2_s, r2_r, o_s, o_r,
):
    r, c = lax.axis_index("row"), lax.axis_index("col")
    z, q = r // 2, r % 2
    sib = r + 1 - 2 * q
    sf, ss = 1 + 3 * q, 4 - 3 * q
    f, s = (c // sf) % 4, (c // ss) % 4
    place = 4 * s + f

    def slot(cc):
        return 4 * ((cc // sf) % 4) + (cc // ss) % 4

    def col_of(ff, sx):
        return ff * sf + sx * ss

    def remote(src, dst, send, recv, row, colm):
        return pltpu.make_async_remote_copy(
            src_ref=src, dst_ref=dst, send_sem=send, recv_sem=recv, device_id=(row, colm), device_id_type=MESH
        )

    def wait_bytes(ref, sem):
        pltpu.make_async_copy(ref, ref, sem).wait()

    e_copy = pltpu.make_async_copy(e_hbm.at[:, pl.ds(pl.multiple_of(16 * c, 16), 16), :], ebuf, e_sem)
    e_copy.start()

    barrier = pltpu.get_barrier_semaphore()

    def greet(d, carry):
        pl.semaphore_signal(barrier, inc=1, device_id=((r + d) % 16, c), device_id_type=MESH)
        pl.semaphore_signal(barrier, inc=1, device_id=(r, (c + d) % 16), device_id_type=MESH)
        return carry

    lax.fori_loop(1, 16, greet, 0)

    @pl.when(r < 4)
    def _():
        band[0, r] = a_ref[0, 0:256, :]
        band[1, r] = a_ref[1, 0:256, :]

    pl.semaphore_wait(barrier, 30)

    def chain(h, i):
        pos = z if h == 0 else (9 - z) % 8
        nxt, prv = ((z + 1) % 8, (z + 7) % 8) if h == 0 else ((z + 7) % 8, (z + 1) % 8)
        is_a = (i // 4 + jnp.where(pos == 0, 1, 0)) % 2
        tile = (q + 2 - 2 * is_a) if h == 0 else (q + 2 * is_a)
        other = (1 - q + 2 - 2 * is_a) if h == 0 else (1 - q + 2 * is_a)
        k = i % 4
        n = 8 * h + 4 * is_a + k
        rows = pl.ds(pl.multiple_of(64 * k, 64), 64)
        mine, theirs = band.at[h, tile, rows], band.at[h, other, rows]
        fwd = remote(mine, mine, ring_s.at[n], ring_r.at[n], 2 * nxt + q, c)
        back = remote(mine, mine, back_s.at[4 * h + k], ring_r.at[n], 2 * prv + q, c)
        to_sib = remote(mine, mine, sib_s.at[n], sib_r.at[n], sib, c)
        from_sib = remote(theirs, theirs, sib_s.at[n], sib_r.at[n], sib, c)
        origin = pos == 1 - is_a
        forwards = jnp.logical_and(pos < 7, pos + is_a > 0)
        returns = jnp.logical_and(pos == 1, is_a == 0)
        return fwd, back, to_sib, from_sib, origin, forwards, returns

    def ring_step(i, carry):
        for h in (0, 1):
            fwd, back, to_sib, _, origin, forwards, returns = chain(h, i)

            @pl.when(jnp.logical_not(origin))
            def _():
                fwd.wait_recv()

            @pl.when(forwards)
            def _():
                fwd.start()

            @pl.when(returns)
            def _():
                back.start()

            to_sib.start()
        return carry

    lax.fori_loop(0, 8, ring_step, 0)

    def ring_end(i, carry):
        for h in (0, 1):
            fwd, back, to_sib, from_sib, origin, forwards, returns = chain(h, i)

            @pl.when(forwards)
            def _():
                fwd.wait_send()

            @pl.when(returns)
            def _():
                back.wait_send()

            to_sib.wait_send()
            from_sib.wait_recv()
        return carry

    lax.fori_loop(0, 8, ring_end, 0)

    def product(i, carry):
        n, tl = i // 2, i % 2
        rows = pl.ds(pl.multiple_of(256 * tl, 256), 256)
        res = dot_nt(a_ref[0, rows, :], band[0, n]) + dot_nt(a_ref[1, rows, :], band[1, n])
        for cc in range(16):
            part[slot(cc), n, pl.ds(pl.multiple_of(16 * tl, 16), 16), :] = res[16 * cc : 16 * cc + 16]
        return carry

    lax.fori_loop(0, 8, product, 0)
    e_copy.wait()

    def d_send(u, d):
        cc = (c + d) % 16
        return remote(part.at[slot(cc), u, pl.ds(0, 16)], drs.at[u, d - 1], d_s.at[u], d_r.at[u], r, cc)

    for u in range(4):

        @pl.when(jnp.logical_and(r < 4, u <= r))
        def _():
            def one(d, carry):
                d_send(u, d).start()
                return carry

            lax.fori_loop(1, 16, one, 0)

    own_rows = pl.ds(pl.multiple_of(16 * place, 16), 16)
    for u in range(4):

        @pl.when(jnp.logical_and(r < 4, u <= r))
        def _():
            wait_bytes(drs.at[u], d_r.at[u])
            total = part[slot(c), u, 0:16, :]
            for k in range(15):
                total = total + drs[u, k]
            dt[r, u, own_rows, :] = ebuf[0, :, 256 * u : 256 * u + 256] - total
            piece = dt.at[r, u, own_rows]

            def one(d, carry):
                remote(piece, piece, z_s.at[u], z_r.at[u // 4 + r // 2, u], 2 * ((z + d) % 8) + q, c).start()
                return carry

            lax.fori_loop(1, 8, one, 0)

    def tiles(fn):
        for tt in (0, 1):
            for u in range(4):
                t = 2 * tt + q

                @pl.when(u <= t)
                def _():
                    fn(tt, t, u)

    def gather1(tt, t, u):
        piece = dt.at[t, u, own_rows]

        @pl.when(r != t)
        def _():
            remote(piece, piece, z_s.at[u], z_r.at[tt, u], sib, c).wait_recv()

        for d in (1, 2, 3):
            remote(piece, piece, g1_s.at[tt, u], g1_r.at[tt, u], r, col_of((f + d) % 4, s)).start()

    line = pl.ds(pl.multiple_of(64 * s, 64), 64)

    def gather2(tt, t, u):
        wait_bytes(dt.at[t, u, pl.ds(0, 48)], g1_r.at[tt, u])
        piece = dt.at[t, u, line]
        for d in (1, 2, 3):
            remote(piece, piece, g2_s.at[tt, u], g2_r.at[tt, u], r, col_of(f, (s + d) % 4)).start()

    def gather3(tt, t, u):
        wait_bytes(dt.at[t, u, pl.ds(0, 192)], g2_r.at[tt, u])
        remote(dt.at[t, u], dt.at[t, u], gs_s.at[tt, u], gs_r.at[tt, u], sib, c).start()

    tiles(gather1)
    tiles(gather2)
    tiles(gather3)
    for t in range(4):
        for u in range(t + 1):

            @pl.when(q != t % 2)
            def _():
                wait_bytes(dt.at[t, u], gs_r.at[t // 2, u])

    for d in (1, 2, 3):
        ff = (f + d) % 4
        remote(part.at[pl.ds(4 * ff, 4)], rs1.at[d - 1], r1_s, r1_r, r, col_of(ff, s)).start()

    def sum_first():
        wait_bytes(rs1, r1_r)
        for u in range(4):

            @pl.when(jnp.logical_and(r < 4, u <= r))
            def _():
                wait_bytes(drs.at[u], d_s.at[u])

        def one(i, carry):
            k, n = i // 4, i % 4
            part[4 * f + k, n] = part[4 * f + k, n] + (rs1[0, k, n] + rs1[1, k, n] + rs1[2, k, n])
            return carry

        lax.fori_loop(0, 16, one, 0)
        for d in (1, 2, 3):
            sx = (s + d) % 4
            remote(part.at[4 * f + sx], rs2.at[d - 1], r2_s, r2_r, r, col_of(f, sx)).start()

    def sum_second():
        wait_bytes(rs2, r2_r)
        for n in range(4):
            total = part[4 * f + s, n] + (rs2[0, n] + rs2[1, n] + rs2[2, n])
            for tl in (0, 1):
                cm[1024 + 16 * tl : 1040 + 16 * tl, 256 * n : 256 * n + 256] = (
                    ebuf[tl, :, 256 * n : 256 * n + 256] - total[16 * tl : 16 * tl + 16]
                )

    for t in range(4):
        for u in range(t + 1):
            for k in range(16):
                at = k if t % 2 == 0 else (k % 4) * 4 + k // 4
                cm[256 * t + 16 * k : 256 * t + 16 * k + 16, 256 * u : 256 * u + 256] = dt[t, u, 16 * at : 16 * at + 16, :]

    def solve_rows(j):
        x = dot_nt(cm[1024:1056, BLK * j : BLK * j + BLK], winv[j])
        cm[1024:1056, BLK * j : BLK * j + BLK] = x
        if j < NB - 1:
            below = BLK * (j + 1)
            cm[1024:1056, below:1024] = cm[1024:1056, below:1024] - dot_nt(x, cm[below:1024, BLK * j : BLK * j + BLK])

    late = 4

    def block(j, carry):
        cols = pl.ds(pl.multiple_of(BLK * j, BLK), BLK)

        def read(i):
            return cm[pl.ds(pl.multiple_of(BLK * j + 8 * i, 8), 8), cols]

        def write(g, x):
            winv[j, 8 * g : 8 * g + 8, :] = x

        factor_inverse(read, write)
        for n in range(NB):

            @pl.when(j == n)
            def _():
                if n == 2:
                    sum_first()
                if n == late:
                    sum_second()
                    for k in range(late):
                        solve_rows(k)
                top, end = BLK * (n + 1), (1056 if n >= late else 1024)
                x = dot_nt(cm[top:end, BLK * n : BLK * n + BLK], winv[n])
                cm[top:end, BLK * n : BLK * n + BLK] = x
                for kb in range(top, 1024, 256):
                    width = min(256, 1024 - kb)
                    cm[kb:end, kb : kb + width] = cm[kb:end, kb : kb + width] - dot_nt(
                        x[kb - top :], x[kb - top : kb - top + width]
                    )

        return carry

    lax.fori_loop(0, NB, block, 0)

    step = lax.broadcasted_iota(jnp.int32, (16, 64), 0)
    lanes = lax.broadcasted_iota(jnp.int32, (16, 64), 1)
    for tl in (0, 1):
        g0 = (16 * tl + r) * 256 + 16 * c
        for cc in range(16):
            x = cm[1024 + 16 * tl : 1040 + 16 * tl, 64 * cc : 64 * cc + 64]
            stage[cc, tl] = jnp.where(lanes + 64 * cc <= step + g0, x, 0.0)
    my_rows = pl.ds(pl.multiple_of(16 * c, 16), 16)

    def out_send(d):
        cc = (c + d) % 16
        return remote(stage.at[cc], outv.at[:, my_rows], o_s.at[d - 1], o_r.at[d - 1], r, cc)

    def out_start(d, carry):
        out_send(d).start()
        return carry

    lax.fori_loop(1, 16, out_start, 0)
    outv[:, my_rows] = stage[c]

    def sent_u(u):
        wait_bytes(dt.at[0, 0, pl.ds(0, 112)], z_s.at[u])

    for u in range(4):

        @pl.when(jnp.logical_and(r < 4, u <= r))
        def _():
            sent_u(u)

    def sent_t(tt, t, u):
        wait_bytes(dt.at[t, u, pl.ds(0, 48)], g1_s.at[tt, u])
        wait_bytes(dt.at[t, u, pl.ds(0, 192)], g2_s.at[tt, u])
        wait_bytes(dt.at[t, u], gs_s.at[tt, u])

    tiles(sent_t)
    wait_bytes(rs1, r1_s)
    wait_bytes(rs2, r2_s)

    def out_end(d, carry):
        copy = out_send(d)
        copy.wait_send()
        copy.wait_recv()
        return carry

    lax.fori_loop(1, 16, out_end, 0)
    out_ref[...] = outv[...]


def per_device(old_factor, panel_block):
    a = jnp.stack([old_factor[:, :, 0, :].reshape(512, 256), old_factor[:, :, 1, :].reshape(512, 256)])
    dma = pltpu.SemaphoreType.DMA
    scratch = [
        pltpu.VMEM((2, 4, 256, 256), F32),
        pltpu.VMEM((16, 4, 32, 256), F32),
        pltpu.VMEM((3, 4, 4, 32, 256), F32),
        pltpu.VMEM((3, 4, 32, 256), F32),
        pltpu.VMEM((4, 15, 16, 256), F32),
        pltpu.VMEM((4, 4, 256, 256), F32),
        pltpu.VMEM((1056, 1024), F32),
        pltpu.VMEM((NB, BLK, BLK), F32),
        pltpu.VMEM((16, 2, 16, 64), F32),
        pltpu.VMEM((2, 256, 64), F32),
        pltpu.VMEM((2, 16, 1024), F32),
        dma, dma((16,)), dma((16,)), dma((8,)), dma((16,)), dma((16,)),
        dma((4,)), dma((4,)), dma((4,)), dma((2, 4)), dma((2, 4)), dma((2, 4)), dma((2, 4)), dma((2, 4)), dma((2, 4)), dma((2, 4)),
        dma, dma, dma, dma, dma((15,)), dma((15,)),
    ]
    return pl.pallas_call(
        kernel,
        out_shape=jax.ShapeDtypeStruct((2, 256, 64), F32),
        in_specs=[pl.BlockSpec(memory_space=pltpu.VMEM), pl.BlockSpec(memory_space=pl.ANY)],
        out_specs=pl.BlockSpec(memory_space=pltpu.VMEM),
        scratch_shapes=scratch,
        compiler_params=pltpu.CompilerParams(
            collective_id=0, has_side_effects=True, vmem_limit_bytes=48 * 1024 * 1024
        ),
    )(a, panel_block)


def solution(mesh):
    return jax.shard_map(
        per_device,
        mesh=mesh,
        in_specs=(P(None, "row", None, "col"), P(None, "row", None)),
        out_specs=P(None, "row", "col"),
        check_vma=False,
    )
```

```python
import jax
import jax.numpy as jnp
from jax import lax
from jax.experimental import pallas as pl
from jax.experimental.pallas import tpu as pltpu
from jax.sharding import PartitionSpec as P

F32 = jnp.float32
MESH = pl.DeviceIdType.MESH
BLK = 128
NB = 8
SUPER = 2


def lane(x, k):
    return jnp.broadcast_to(x[:, k : k + 1], (8, BLK))


def sub(x, k):
    return jnp.broadcast_to(x[k : k + 1, :], (8, BLK))


def dot_tn(a, b):
    return lax.dot_general(
        a, b, (((0,), (0,)), ((), ())), precision=lax.Precision.HIGHEST, preferred_element_type=F32
    )


def dot_nt(a, b):
    return lax.dot_general(
        a, b, (((1,), (1,)), ((), ())), precision=lax.Precision.HIGHEST, preferred_element_type=F32
    )


def factor_inverse(read, write):
    idx = lax.broadcasted_iota(jnp.int32, (8, BLK), 0)
    col = lax.broadcasted_iota(jnp.int32, (8, BLK), 1)
    groups = BLK // 8
    m = [read(i) for i in range(groups)]
    w = [jnp.where(col == idx + 8 * i, 1.0, 0.0).astype(F32) for i in range(groups)]
    u = [None] * groups
    uw = [None] * groups
    for g in range(groups):
        sb = g // SUPER
        near = list(range(g + 1, min(groups, SUPER * (sb + 2))))
        t, v = m[g], w[g]
        piv = [lane(t, 8 * g + k) for k in range(8)]
        low = {i: [lane(m[i], 8 * g + k) for k in range(8)] for i in near}
        rows, rows_w, mult = [], [], {i: [] for i in near}
        for k in range(8):
            scale = lax.rsqrt(sub(piv[k], k))
            mk = jnp.where(idx > k, piv[k] * scale, 0.0)
            rk, rwk = sub(t, k) * scale, sub(v, k) * scale
            rows.append(rk)
            rows_w.append(rwk)
            if k < 7:
                t, v = t - mk * rk, v - mk * rwk
            for i in near:
                mult[i].append(low[i][k] * scale)
            for n in range(k + 1, 8):
                q = sub(piv[n], k) * scale
                piv[n] = piv[n] - mk * q
                for i in near:
                    low[i][n] = low[i][n] - mult[i][k] * q
        ug, uwg = rows[0], rows_w[0]
        for k in range(1, 8):
            ug, uwg = jnp.where(idx == k, rows[k], ug), jnp.where(idx == k, rows_w[k], uwg)
        u[g], uw[g] = ug, uwg
        write(g, uwg)
        for i in near:
            a, b = m[i], w[i]
            for k in range(8):
                a, b = a - mult[i][k] * rows[k], b - mult[i][k] * rows_w[k]
            m[i], w[i] = a, b
        first = SUPER * (sb + 2)
        if g % SUPER == SUPER - 1 and first < groups:
            us = jnp.concatenate(u[SUPER * sb : g + 1], axis=0)
            ws = jnp.concatenate(uw[SUPER * sb : g + 1], axis=0)
            eu, ew = dot_tn(us, us), dot_tn(us, ws)
            for i in range(first, groups):
                m[i], w[i] = m[i] - eu[8 * i : 8 * i + 8], w[i] - ew[8 * i : 8 * i + 8]


def kernel(
    a_ref, e_hbm, out_ref,
    band, part, rs1, rs2, drs, dt, cm, winv, stage, outv, ebuf,
    e_sem, ring_s, ring_r, back_s, sib_s, sib_r,
    d_s, d_r, z_s, z_r, g1_s, g1_r, g2_s, g2_r, gs_s, gs_r,
    r1_s, r1_r, r2_s, r2_r, o_s, o_r,
):
    r, c = lax.axis_index("row"), lax.axis_index("col")
    z, q = r // 2, r % 2
    sib = r + 1 - 2 * q
    sf, ss = 1 + 3 * q, 4 - 3 * q
    f, s = (c // sf) % 4, (c // ss) % 4
    place = 4 * s + f

    def slot(cc):
        return 4 * ((cc // sf) % 4) + (cc // ss) % 4

    def col_of(ff, sx):
        return ff * sf + sx * ss

    def remote(src, dst, send, recv, row, colm):
        return pltpu.make_async_remote_copy(
            src_ref=src, dst_ref=dst, send_sem=send, recv_sem=recv, device_id=(row, colm), device_id_type=MESH
        )

    def wait_bytes(ref, sem):
        pltpu.make_async_copy(ref, ref, sem).wait()

    e_copy = pltpu.make_async_copy(e_hbm.at[:, pl.ds(pl.multiple_of(16 * c, 16), 16), :], ebuf, e_sem)
    e_copy.start()

    barrier = pltpu.get_barrier_semaphore()

    def greet(d, carry):
        pl.semaphore_signal(barrier, inc=1, device_id=((r + d) % 16, c), device_id_type=MESH)
        pl.semaphore_signal(barrier, inc=1, device_id=(r, (c + d) % 16), device_id_type=MESH)
        return carry

    lax.fori_loop(1, 16, greet, 0)

    @pl.when(r < 4)
    def _():
        band[0, r] = a_ref[0, 0:256, :]
        band[1, r] = a_ref[1, 0:256, :]

    pl.semaphore_wait(barrier, 30)

    def chain(h, i):
        pos = z if h == 0 else (9 - z) % 8
        nxt, prv = ((z + 1) % 8, (z + 7) % 8) if h == 0 else ((z + 7) % 8, (z + 1) % 8)
        is_a = (i // 4 + jnp.where(pos == 0, 1, 0)) % 2
        tile = (q + 2 - 2 * is_a) if h == 0 else (q + 2 * is_a)
        other = (1 - q + 2 - 2 * is_a) if h == 0 else (1 - q + 2 * is_a)
        k = i % 4
        n = 8 * h + 4 * is_a + k
        rows = pl.ds(pl.multiple_of(64 * k, 64), 64)
        mine, theirs = band.at[h, tile, rows], band.at[h, other, rows]
        fwd = remote(mine, mine, ring_s.at[n], ring_r.at[n], 2 * nxt + q, c)
        back = remote(mine, mine, back_s.at[4 * h + k], ring_r.at[n], 2 * prv + q, c)
        to_sib = remote(mine, mine, sib_s.at[n], sib_r.at[n], sib, c)
        from_sib = remote(theirs, theirs, sib_s.at[n], sib_r.at[n], sib, c)
        origin = pos == 1 - is_a
        forwards = jnp.logical_and(pos < 7, pos + is_a > 0)
        returns = jnp.logical_and(pos == 1, is_a == 0)
        return fwd, back, to_sib, from_sib, origin, forwards, returns

    def ring_step(tick, carry):
        for h in (0, 1):
            pos = z if h == 0 else (9 - z) % 8
            late_by = jnp.maximum(pos - 1, 0)
            i = jnp.clip(tick - late_by, 0, 7)

            @pl.when(jnp.logical_and(tick >= late_by, tick < late_by + 8))
            def _():
                fwd, back, to_sib, _, origin, forwards, returns = chain(h, i)

                @pl.when(jnp.logical_not(origin))
                def _():
                    fwd.wait_recv()

                @pl.when(forwards)
                def _():
                    fwd.start()

                @pl.when(returns)
                def _():
                    back.start()

                to_sib.start()

        return carry

    lax.fori_loop(0, 14, ring_step, 0)

    def ring_end(i, carry):
        for h in (0, 1):
            fwd, back, to_sib, from_sib, origin, forwards, returns = chain(h, i)

            @pl.when(forwards)
            def _():
                fwd.wait_send()

            @pl.when(returns)
            def _():
                back.wait_send()

            to_sib.wait_send()
            from_sib.wait_recv()
        return carry

    lax.fori_loop(0, 8, ring_end, 0)

    def product(i, carry):
        n, tl = i // 2, i % 2
        rows = pl.ds(pl.multiple_of(256 * tl, 256), 256)
        res = dot_nt(a_ref[0, rows, :], band[0, n]) + dot_nt(a_ref[1, rows, :], band[1, n])
        for cc in range(16):
            part[slot(cc), n, pl.ds(pl.multiple_of(16 * tl, 16), 16), :] = res[16 * cc : 16 * cc + 16]
        return carry

    lax.fori_loop(0, 8, product, 0)
    e_copy.wait()

    def d_send(u, d):
        cc = (c + d) % 16
        return remote(part.at[slot(cc), u, pl.ds(0, 16)], drs.at[u, d - 1], d_s.at[u], d_r.at[u], r, cc)

    for u in range(4):

        @pl.when(jnp.logical_and(r < 4, u <= r))
        def _():
            def one(d, carry):
                d_send(u, d).start()
                return carry

            lax.fori_loop(1, 16, one, 0)

    own_rows = pl.ds(pl.multiple_of(16 * place, 16), 16)
    for u in range(4):

        @pl.when(jnp.logical_and(r < 4, u <= r))
        def _():
            wait_bytes(drs.at[u], d_r.at[u])
            total = part[slot(c), u, 0:16, :]
            for k in range(15):
                total = total + drs[u, k]
            dt[r, u, own_rows, :] = ebuf[0, :, 256 * u : 256 * u + 256] - total
            piece = dt.at[r, u, own_rows]

            def one(d, carry):
                remote(piece, piece, z_s.at[u], z_r.at[u // 4 + r // 2, u], 2 * ((z + d) % 8) + q, c).start()
                return carry

            lax.fori_loop(1, 8, one, 0)

    def tiles(fn):
        for tt in (0, 1):
            for u in range(4):
                t = 2 * tt + q

                @pl.when(u <= t)
                def _():
                    fn(tt, t, u)

    def gather1(tt, t, u):
        piece = dt.at[t, u, own_rows]

        @pl.when(r != t)
        def _():
            remote(piece, piece, z_s.at[u], z_r.at[tt, u], sib, c).wait_recv()

        for d in (1, 2, 3):
            remote(piece, piece, g1_s.at[tt, u], g1_r.at[tt, u], r, col_of((f + d) % 4, s)).start()

    line = pl.ds(pl.multiple_of(64 * s, 64), 64)

    def gather2(tt, t, u):
        wait_bytes(dt.at[t, u, pl.ds(0, 48)], g1_r.at[tt, u])
        piece = dt.at[t, u, line]
        for d in (1, 2, 3):
            remote(piece, piece, g2_s.at[tt, u], g2_r.at[tt, u], r, col_of(f, (s + d) % 4)).start()

    def gather3(tt, t, u):
        wait_bytes(dt.at[t, u, pl.ds(0, 192)], g2_r.at[tt, u])
        remote(dt.at[t, u], dt.at[t, u], gs_s.at[tt, u], gs_r.at[tt, u], sib, c).start()

    tiles(gather1)
    tiles(gather2)
    tiles(gather3)
    for t in range(4):
        for u in range(t + 1):

            @pl.when(q != t % 2)
            def _():
                wait_bytes(dt.at[t, u], gs_r.at[t // 2, u])

    for d in (1, 2, 3):
        ff = (f + d) % 4
        remote(part.at[pl.ds(4 * ff, 4)], rs1.at[d - 1], r1_s, r1_r, r, col_of(ff, s)).start()

    def sum_first():
        wait_bytes(rs1, r1_r)
        for u in range(4):

            @pl.when(jnp.logical_and(r < 4, u <= r))
            def _():
                wait_bytes(drs.at[u], d_s.at[u])

        def one(i, carry):
            k, n = i // 4, i % 4
            part[4 * f + k, n] = part[4 * f + k, n] + (rs1[0, k, n] + rs1[1, k, n] + rs1[2, k, n])
            return carry

        lax.fori_loop(0, 16, one, 0)
        for d in (1, 2, 3):
            sx = (s + d) % 4
            remote(part.at[4 * f + sx], rs2.at[d - 1], r2_s, r2_r, r, col_of(f, sx)).start()

    def sum_second():
        wait_bytes(rs2, r2_r)
        for n in range(4):
            total = part[4 * f + s, n] + (rs2[0, n] + rs2[1, n] + rs2[2, n])
            for tl in (0, 1):
                cm[1024 + 16 * tl : 1040 + 16 * tl, 256 * n : 256 * n + 256] = (
                    ebuf[tl, :, 256 * n : 256 * n + 256] - total[16 * tl : 16 * tl + 16]
                )

    for t in range(4):
        for u in range(t + 1):
            for k in range(16):
                at = k if t % 2 == 0 else (k % 4) * 4 + k // 4
                cm[256 * t + 16 * k : 256 * t + 16 * k + 16, 256 * u : 256 * u + 256] = dt[t, u, 16 * at : 16 * at + 16, :]

    def solve_rows(j):
        x = dot_nt(cm[1024:1056, BLK * j : BLK * j + BLK], winv[j])
        cm[1024:1056, BLK * j : BLK * j + BLK] = x
        if j < NB - 1:
            below = BLK * (j + 1)
            cm[1024:1056, below:1024] = cm[1024:1056, below:1024] - dot_nt(x, cm[below:1024, BLK * j : BLK * j + BLK])

    late = 4

    def block(j, carry):
        cols = pl.ds(pl.multiple_of(BLK * j, BLK), BLK)

        def read(i):
            return cm[pl.ds(pl.multiple_of(BLK * j + 8 * i, 8), 8), cols]

        def write(g, x):
            winv[j, 8 * g : 8 * g + 8, :] = x

        factor_inverse(read, write)
        for n in range(NB):

            @pl.when(j == n)
            def _():
                if n == 2:
                    sum_first()
                if n == late:
                    sum_second()
                    for k in range(late):
                        solve_rows(k)
                top, end = BLK * (n + 1), (1056 if n >= late else 1024)
                x = dot_nt(cm[top:end, BLK * n : BLK * n + BLK], winv[n])
                cm[top:end, BLK * n : BLK * n + BLK] = x
                for kb in range(top, 1024, 256):
                    width = min(256, 1024 - kb)
                    cm[kb:end, kb : kb + width] = cm[kb:end, kb : kb + width] - dot_nt(
                        x[kb - top :], x[kb - top : kb - top + width]
                    )

        return carry

    lax.fori_loop(0, NB, block, 0)

    step = lax.broadcasted_iota(jnp.int32, (16, 64), 0)
    lanes = lax.broadcasted_iota(jnp.int32, (16, 64), 1)
    for tl in (0, 1):
        g0 = (16 * tl + r) * 256 + 16 * c
        for cc in range(16):
            x = cm[1024 + 16 * tl : 1040 + 16 * tl, 64 * cc : 64 * cc + 64]
            stage[cc, tl] = jnp.where(lanes + 64 * cc <= step + g0, x, 0.0)
    my_rows = pl.ds(pl.multiple_of(16 * c, 16), 16)

    def out_send(d):
        cc = (c + d) % 16
        return remote(stage.at[cc], outv.at[:, my_rows], o_s.at[d - 1], o_r.at[d - 1], r, cc)

    def out_start(d, carry):
        out_send(d).start()
        return carry

    lax.fori_loop(1, 16, out_start, 0)
    outv[:, my_rows] = stage[c]

    def sent_u(u):
        wait_bytes(dt.at[0, 0, pl.ds(0, 112)], z_s.at[u])

    for u in range(4):

        @pl.when(jnp.logical_and(r < 4, u <= r))
        def _():
            sent_u(u)

    def sent_t(tt, t, u):
        wait_bytes(dt.at[t, u, pl.ds(0, 48)], g1_s.at[tt, u])
        wait_bytes(dt.at[t, u, pl.ds(0, 192)], g2_s.at[tt, u])
        wait_bytes(dt.at[t, u], gs_s.at[tt, u])

    tiles(sent_t)
    wait_bytes(rs1, r1_s)
    wait_bytes(rs2, r2_s)

    def out_end(d, carry):
        copy = out_send(d)
        copy.wait_send()
        copy.wait_recv()
        return carry

    lax.fori_loop(1, 16, out_end, 0)
    out_ref[...] = outv[...]


def per_device(old_factor, panel_block):
    a = jnp.stack([old_factor[:, :, 0, :].reshape(512, 256), old_factor[:, :, 1, :].reshape(512, 256)])
    dma = pltpu.SemaphoreType.DMA
    scratch = [
        pltpu.VMEM((2, 4, 256, 256), F32),
        pltpu.VMEM((16, 4, 32, 256), F32),
        pltpu.VMEM((3, 4, 4, 32, 256), F32),
        pltpu.VMEM((3, 4, 32, 256), F32),
        pltpu.VMEM((4, 15, 16, 256), F32),
        pltpu.VMEM((4, 4, 256, 256), F32),
        pltpu.VMEM((1056, 1024), F32),
        pltpu.VMEM((NB, BLK, BLK), F32),
        pltpu.VMEM((16, 2, 16, 64), F32),
        pltpu.VMEM((2, 256, 64), F32),
        pltpu.VMEM((2, 16, 1024), F32),
        dma, dma((16,)), dma((16,)), dma((8,)), dma((16,)), dma((16,)),
        dma((4,)), dma((4,)), dma((4,)), dma((2, 4)), dma((2, 4)), dma((2, 4)), dma((2, 4)), dma((2, 4)), dma((2, 4)), dma((2, 4)),
        dma, dma, dma, dma, dma((15,)), dma((15,)),
    ]
    return pl.pallas_call(
        kernel,
        out_shape=jax.ShapeDtypeStruct((2, 256, 64), F32),
        in_specs=[pl.BlockSpec(memory_space=pltpu.VMEM), pl.BlockSpec(memory_space=pl.ANY)],
        out_specs=pl.BlockSpec(memory_space=pltpu.VMEM),
        scratch_shapes=scratch,
        compiler_params=pltpu.CompilerParams(
            collective_id=0, has_side_effects=True, vmem_limit_bytes=48 * 1024 * 1024
        ),
    )(a, panel_block)


def solution(mesh):
    return jax.shard_map(
        per_device,
        mesh=mesh,
        in_specs=(P(None, "row", None, "col"), P(None, "row", None)),
        out_specs=P(None, "row", "col"),
        check_vma=False,
    )
```

```python
import jax
import jax.numpy as jnp
from jax import lax
from jax.experimental import pallas as pl
from jax.experimental.pallas import tpu as pltpu
from jax.sharding import PartitionSpec as P

F32 = jnp.float32
MESH = pl.DeviceIdType.MESH
BLK = 128
NB = 8
SUPER = 2
NCH = 4
LAG = 3


def lane(x, k):
    return jnp.broadcast_to(x[:, k : k + 1], (8, BLK))


def sub(x, k):
    return jnp.broadcast_to(x[k : k + 1, :], (8, BLK))


def dot_tn(a, b):
    return lax.dot_general(
        a, b, (((0,), (0,)), ((), ())), precision=lax.Precision.HIGHEST, preferred_element_type=F32
    )


def dot_nt(a, b):
    return lax.dot_general(
        a, b, (((1,), (1,)), ((), ())), precision=lax.Precision.HIGHEST, preferred_element_type=F32
    )


def factor_inverse(read, write, poll=None):
    idx = lax.broadcasted_iota(jnp.int32, (8, BLK), 0)
    col = lax.broadcasted_iota(jnp.int32, (8, BLK), 1)
    groups = BLK // 8
    m = [read(i) for i in range(groups)]
    w = [jnp.where(col == idx + 8 * i, 1.0, 0.0).astype(F32) for i in range(groups)]
    u = [None] * groups
    uw = [None] * groups
    for g in range(groups):
        sb = g // SUPER
        near = list(range(g + 1, min(groups, SUPER * (sb + 2))))
        t, v = m[g], w[g]
        piv = [lane(t, 8 * g + k) for k in range(8)]
        low = {i: [lane(m[i], 8 * g + k) for k in range(8)] for i in near}
        rows, rows_w, mult = [], [], {i: [] for i in near}
        for k in range(8):
            scale = lax.rsqrt(sub(piv[k], k))
            mk = jnp.where(idx > k, piv[k] * scale, 0.0)
            rk, rwk = sub(t, k) * scale, sub(v, k) * scale
            rows.append(rk)
            rows_w.append(rwk)
            if k < 7:
                t, v = t - mk * rk, v - mk * rwk
            for i in near:
                mult[i].append(low[i][k] * scale)
            for n in range(k + 1, 8):
                q = sub(piv[n], k) * scale
                piv[n] = piv[n] - mk * q
                for i in near:
                    low[i][n] = low[i][n] - mult[i][k] * q
        ug, uwg = rows[0], rows_w[0]
        for k in range(1, 8):
            ug, uwg = jnp.where(idx == k, rows[k], ug), jnp.where(idx == k, rows_w[k], uwg)
        u[g], uw[g] = ug, uwg
        write(g, uwg)
        for i in near:
            a, b = m[i], w[i]
            for k in range(8):
                a, b = a - mult[i][k] * rows[k], b - mult[i][k] * rows_w[k]
            m[i], w[i] = a, b
        if poll is not None and g % 4 == 3:
            poll(g // 4)
        first = SUPER * (sb + 2)
        if g % SUPER == SUPER - 1 and first < groups:
            us = jnp.concatenate(u[SUPER * sb : g + 1], axis=0)
            ws = jnp.concatenate(uw[SUPER * sb : g + 1], axis=0)
            eu, ew = dot_tn(us, us), dot_tn(us, ws)
            for i in range(first, groups):
                m[i], w[i] = m[i] - eu[8 * i : 8 * i + 8], w[i] - ew[8 * i : 8 * i + 8]


def kernel(
    a_ref, e_hbm, out_ref,
    band, part, rs1, rs2, dpart, drs, cm, winv, stage, outv, ebuf,
    e_sem, ring_s, ring_r, back_s, sib_s, sib_r,
    d_s, d_r, z_s, z_r, g_s, g_r, gs_s, gs_r,
    r1_s, r1_r, r2_s, r2_r, o_s, o_r,
):
    r, c = lax.axis_index("row"), lax.axis_index("col")
    z, q = r // 2, r % 2
    sib = r + 1 - 2 * q
    sf, ss = 1 + 3 * q, 4 - 3 * q
    f, s = (c // sf) % 4, (c // ss) % 4

    def slot(cc):
        return 4 * ((cc // sf) % 4) + (cc // ss) % 4

    def col_of(ff, sx):
        return ff * sf + sx * ss

    def remote(src, dst, send, recv, row, colm):
        return pltpu.make_async_remote_copy(
            src_ref=src, dst_ref=dst, send_sem=send, recv_sem=recv, device_id=(row, colm), device_id_type=MESH
        )

    def wait_bytes(ref, sem):
        pltpu.make_async_copy(ref, ref, sem).wait()

    e_copy = pltpu.make_async_copy(e_hbm.at[:, pl.ds(pl.multiple_of(16 * c, 16), 16), :], ebuf, e_sem)
    e_copy.start()

    barrier = pltpu.get_barrier_semaphore()

    def greet(d, carry):
        pl.semaphore_signal(barrier, inc=1, device_id=(r, (c + d) % 16), device_id_type=MESH)
        return carry

    pl.semaphore_signal(barrier, inc=1, device_id=(sib, c), device_id_type=MESH)
    for d in range(1, 8):
        pl.semaphore_signal(barrier, inc=1, device_id=(2 * ((z + d) % 8) + q, c), device_id_type=MESH)
    lax.fori_loop(1, 16, greet, 0)

    @pl.when(r < 4)
    def _():
        low, high = a_ref[0, 0:256, :], a_ref[1, 0:256, :]
        band[0, r] = low
        band[1, r] = high
        dpart[r] = dot_nt(low, low) + dot_nt(high, high)

    e_copy.wait()
    pl.semaphore_wait(barrier, 23)

    def chain(h, i):
        pos = z if h == 0 else (9 - z) % 8
        nxt, prv = ((z + 1) % 8, (z + 7) % 8) if h == 0 else ((z + 7) % 8, (z + 1) % 8)
        is_a = (i // NCH + jnp.where(pos == 0, 1, 0)) % 2
        tile = (q + 2 - 2 * is_a) if h == 0 else (q + 2 * is_a)
        k = i % NCH
        n = 2 * NCH * h + NCH * is_a + k
        mine = band.at[h, tile, pl.ds(pl.multiple_of(256 // NCH * k, 256 // NCH), 256 // NCH)]
        fwd = remote(mine, mine, ring_s.at[n], ring_r.at[n], 2 * nxt + q, c)
        back = remote(mine, mine, back_s.at[NCH * h + k], ring_r.at[n], 2 * prv + q, c)
        to_sib = remote(mine, mine, sib_s.at[n], sib_r.at[n], sib, c)
        origin = pos == 1 - is_a
        forwards = jnp.logical_and(pos < 7, pos + is_a > 0)
        returns = jnp.logical_and(pos == 1, is_a == 0)
        return fwd, back, to_sib, origin, forwards, returns

    def ring_step(tick, carry):
        for h in (0, 1):
            pos = z if h == 0 else (9 - z) % 8
            late_by = LAG * jnp.maximum(pos - 1, 0)
            i = jnp.clip(tick - late_by, 0, 2 * NCH - 1)

            @pl.when(jnp.logical_and(tick >= late_by, tick < late_by + 2 * NCH))
            def _():
                fwd, back, to_sib, origin, forwards, returns = chain(h, i)

                @pl.when(jnp.logical_not(origin))
                def _():
                    fwd.wait_recv()

                @pl.when(forwards)
                def _():
                    fwd.start()

                @pl.when(returns)
                def _():
                    back.start()

                to_sib.start()

        return carry

    def ring(first, last):
        lax.fori_loop(first, last, ring_step, 0)

    def from_sibling(second):
        def one(k, carry):
            for h in (0, 1):
                is_a = 1 - second if h == 0 else second
                n = 2 * NCH * h + NCH * is_a + k
                theirs = band.at[h, 1 - q + 2 * second, pl.ds(pl.multiple_of(256 // NCH * k, 256 // NCH), 256 // NCH)]
                remote(theirs, theirs, sib_s.at[n], sib_r.at[n], sib, c).wait_recv()
            return carry

        lax.fori_loop(0, NCH, one, 0)

    def ring_end():
        def one(i, carry):
            for h in (0, 1):
                fwd, back, to_sib, origin, forwards, returns = chain(h, i)

                @pl.when(forwards)
                def _():
                    fwd.wait_send()

                @pl.when(returns)
                def _():
                    back.wait_send()

                to_sib.wait_send()
            return carry

        lax.fori_loop(0, 2 * NCH, one, 0)

        @pl.when(z > 1)
        def _():
            from_sibling(0)

        @pl.when(z != 1)
        def _():
            from_sibling(1)

    def d_send(u, d):
        cc = (c + d) % 16
        rows = pl.ds(pl.multiple_of(16 * cc, 16), 16)
        return remote(dpart.at[u, rows], drs.at[u, d - 1], d_s.at[u], d_r.at[u], r, cc)

    def d_start(u):
        def one(d, carry):
            d_send(u, d).start()
            return carry

        lax.fori_loop(1, 16, one, 0)

    def d_rest(owner):
        @pl.when(r == owner)
        def _():
            for u in range(owner):
                dpart[u] = dot_nt(a_ref[0, 0:256, :], band[0, u]) + dot_nt(a_ref[1, 0:256, :], band[1, u])
                d_start(u)

    def piece_of(t, u):
        rows = pl.ds(pl.multiple_of(256 * t + 16 * c, 16), 16)
        return cm.at[rows, pl.ds(256 * u, 256)]

    def tile_of(t, u):
        return cm.at[pl.ds(pl.multiple_of(256 * t, 256), 256), pl.ds(256 * u, 256)]

    def rows_of(n):
        return cm.at[pl.ds(0, n), pl.ds(0, 256)]

    def sum_tiles(tt):
        for u in range(2 * tt + 2):

            @pl.when(jnp.logical_and(z == tt, u <= r))
            def _():
                wait_bytes(drs.at[u], d_r.at[u])
                total = dpart[u, pl.ds(pl.multiple_of(16 * c, 16), 16), :]
                for k in range(15):
                    total = total + drs[u, k]
                piece = piece_of(r, u)
                piece[...] = ebuf[0, :, 256 * u : 256 * u + 256] - total

                def one(d, carry):
                    remote(piece, piece, z_s.at[u], z_r.at[tt, u], 2 * ((z + d) % 8) + q, c).start()
                    return carry

                lax.fori_loop(1, 8, one, 0)

    def tiles(tt, fn):
        for u in range(2 * tt + 2):
            t = 2 * tt + q

            @pl.when(u <= t)
            def _():
                fn(tt, t, u)

    def gather(tt, t, u):
        piece = piece_of(t, u)

        @pl.when(r != t)
        def _():
            remote(piece, piece, z_s.at[u], z_r.at[tt, u], sib, c).wait_recv()

        def one(d, carry):
            remote(piece, piece, g_s.at[tt, u], g_r.at[tt, u], r, (c + d) % 16).start()
            return carry

        lax.fori_loop(1, 16, one, 0)

    def share(tt, t, u):
        wait_bytes(rows_of(240), g_r.at[tt, u])
        tile = tile_of(t, u)
        remote(tile, tile, gs_s.at[tt, u], gs_r.at[tt, u], sib, c).start()

    def shared(tt):
        for u in range(2 * tt + 2):
            t = 2 * tt + 1 - q

            @pl.when(u <= t)
            def _():
                wait_bytes(rows_of(256), gs_r.at[tt, u])

    def sent(tt):
        def one(tt, t, u):
            wait_bytes(rows_of(240), g_s.at[tt, u])
            wait_bytes(rows_of(256), gs_s.at[tt, u])

        tiles(tt, one)
        for u in range(2 * tt + 2):

            @pl.when(jnp.logical_and(z == tt, u <= r))
            def _():
                wait_bytes(drs.at[u], d_s.at[u])
                wait_bytes(rows_of(112), z_s.at[u])

    def product(i, carry):
        n, tl = i // 2, i % 2
        rows = pl.ds(pl.multiple_of(256 * tl, 256), 256)
        res = dot_nt(a_ref[0, rows, :], band[0, n]) + dot_nt(a_ref[1, rows, :], band[1, n])
        for cc in range(16):
            part[slot(cc), n, pl.ds(pl.multiple_of(16 * tl, 16), 16), :] = res[16 * cc : 16 * cc + 16]
        return carry

    def products():
        lax.fori_loop(0, 8, product, 0)
        for d in (1, 2, 3):
            ff = (f + d) % 4
            remote(part.at[pl.ds(4 * ff, 4)], rs1.at[d - 1], r1_s, r1_r, r, col_of(ff, s)).start()

    def sum_first():
        wait_bytes(rs1, r1_r)

        def one(i, carry):
            k, n = i // 4, i % 4
            part[4 * f + k, n] = part[4 * f + k, n] + (rs1[0, k, n] + rs1[1, k, n] + rs1[2, k, n])
            return carry

        lax.fori_loop(0, 16, one, 0)
        for d in (1, 2, 3):
            sx = (s + d) % 4
            remote(part.at[4 * f + sx], rs2.at[d - 1], r2_s, r2_r, r, col_of(f, sx)).start()

    def sum_second():
        wait_bytes(rs2, r2_r)
        for n in range(4):
            total = part[4 * f + s, n] + (rs2[0, n] + rs2[1, n] + rs2[2, n])
            for tl in (0, 1):
                cm[1024 + 16 * tl : 1040 + 16 * tl, 256 * n : 256 * n + 256] = (
                    ebuf[tl, :, 256 * n : 256 * n + 256] - total[16 * tl : 16 * tl + 16]
                )

    def solve_rows(j):
        x = dot_nt(cm[1024:1056, BLK * j : BLK * j + BLK], winv[j])
        cm[1024:1056, BLK * j : BLK * j + BLK] = x
        if j < NB - 1:
            below = BLK * (j + 1)
            cm[1024:1056, below:1024] = cm[1024:1056, below:1024] - dot_nt(x, cm[below:1024, BLK * j : BLK * j + BLK])

    def blocks(first, last, bottom, rows_from, ticks, after):
        def block(j, carry):
            cols = pl.ds(pl.multiple_of(BLK * j, BLK), BLK)

            def read(i):
                return cm[pl.ds(pl.multiple_of(BLK * j + 8 * i, 8), 8), cols]

            def write(g, x):
                winv[j, 8 * g : 8 * g + 8, :] = x

            def poll(n):
                ring(ticks + 4 * j + n, ticks + 4 * j + n + 1)

            factor_inverse(read, write, poll if ticks else None)
            for n in range(first, last):

                @pl.when(j == n)
                def _():
                    if n == rows_from:
                        for k in range(n):
                            solve_rows(k)
                    top, end = BLK * (n + 1), (1056 if n >= rows_from else bottom)
                    if top < end:
                        x = dot_nt(cm[top:end, BLK * n : BLK * n + BLK], winv[n])
                        cm[top:end, BLK * n : BLK * n + BLK] = x
                        for kb in range(top, bottom, 256):
                            width = min(256, bottom - kb)
                            cm[kb:end, kb : kb + width] = cm[kb:end, kb : kb + width] - dot_nt(
                                x[kb - top :], x[kb - top : kb - top + width]
                            )
                    after(n)

            return carry

        lax.fori_loop(first, last, block, 0)

    @pl.when(r < 4)
    def _():
        d_start(r)

    ring(0, 4)

    @pl.when(z == 0)
    def _():
        from_sibling(0)

    d_rest(1)
    ring(4, 7)
    sum_tiles(0)
    ring(7, 10)
    tiles(0, gather)

    @pl.when(z == 1)
    def _():
        from_sibling(0)
        from_sibling(1)

    d_rest(2)
    d_rest(3)
    ring(10, 12)
    tiles(0, share)
    ring(12, 14)
    sum_tiles(1)
    shared(0)
    sent(0)

    def after_first(n):
        if n == 0:
            tiles(1, gather)
        if n == 2:
            ring_end()
            products()
            tiles(1, share)
        if n == 3:
            shared(1)
            sent(1)

    blocks(0, 4, 512, NB, 14, after_first)

    for k in range(4):
        x = dot_nt(cm[512:1024, BLK * k : BLK * k + BLK], winv[k])
        cm[512:1024, BLK * k : BLK * k + BLK] = x
        if k < 3:
            below = BLK * (k + 1)
            cm[512:1024, below:512] = cm[512:1024, below:512] - dot_nt(x, cm[below:512, BLK * k : BLK * k + BLK])
    for kb in (512, 768):
        cm[kb:1024, kb : kb + 256] = cm[kb:1024, kb : kb + 256] - dot_nt(cm[kb:1024, 0:512], cm[kb : kb + 256, 0:512])

    def after_second(n):
        if n == 4:
            sum_first()
        if n == 5:
            sum_second()

    blocks(4, 8, 1024, 6, 0, after_second)

    step = lax.broadcasted_iota(jnp.int32, (16, 64), 0)
    lanes = lax.broadcasted_iota(jnp.int32, (16, 64), 1)
    for tl in (0, 1):
        g0 = (16 * tl + r) * 256 + 16 * c
        for cc in range(16):
            x = cm[1024 + 16 * tl : 1040 + 16 * tl, 64 * cc : 64 * cc + 64]
            stage[cc, tl] = jnp.where(lanes + 64 * cc <= step + g0, x, 0.0)
    my_rows = pl.ds(pl.multiple_of(16 * c, 16), 16)

    def out_send(d):
        cc = (c + d) % 16
        return remote(stage.at[cc], outv.at[:, my_rows], o_s.at[d - 1], o_r.at[d - 1], r, cc)

    def out_start(d, carry):
        out_send(d).start()
        return carry

    lax.fori_loop(1, 16, out_start, 0)
    outv[:, my_rows] = stage[c]

    wait_bytes(rs1, r1_s)
    wait_bytes(rs2, r2_s)

    def out_end(d, carry):
        copy = out_send(d)
        copy.wait_send()
        copy.wait_recv()
        return carry

    lax.fori_loop(1, 16, out_end, 0)
    out_ref[...] = outv[...]


def per_device(old_factor, panel_block):
    a = jnp.transpose(old_factor, (2, 0, 1, 3)).reshape(2, 512, 256)
    dma = pltpu.SemaphoreType.DMA
    scratch = [
        pltpu.VMEM((2, 4, 256, 256), F32),
        pltpu.VMEM((16, 4, 32, 256), F32),
        pltpu.VMEM((3, 4, 4, 32, 256), F32),
        pltpu.VMEM((3, 4, 32, 256), F32),
        pltpu.VMEM((4, 256, 256), F32),
        pltpu.VMEM((4, 15, 16, 256), F32),
        pltpu.VMEM((1056, 1024), F32),
        pltpu.VMEM((NB, BLK, BLK), F32),
        pltpu.VMEM((16, 2, 16, 64), F32),
        pltpu.VMEM((2, 256, 64), F32),
        pltpu.VMEM((2, 16, 1024), F32),
        dma, dma((4 * NCH,)), dma((4 * NCH,)), dma((2 * NCH,)), dma((4 * NCH,)), dma((4 * NCH,)),
        dma((4,)), dma((4,)), dma((4,)), dma((2, 4)), dma((2, 4)), dma((2, 4)), dma((2, 4)), dma((2, 4)),
        dma, dma, dma, dma, dma((15,)), dma((15,)),
    ]
    return pl.pallas_call(
        kernel,
        out_shape=jax.ShapeDtypeStruct((2, 256, 64), F32),
        in_specs=[pl.BlockSpec(memory_space=pltpu.VMEM), pl.BlockSpec(memory_space=pl.ANY)],
        out_specs=pl.BlockSpec(memory_space=pltpu.VMEM),
        scratch_shapes=scratch,
        compiler_params=pltpu.CompilerParams(
            collective_id=0, has_side_effects=True, vmem_limit_bytes=60 * 1024 * 1024
        ),
    )(a, panel_block)


def solution(mesh):
    return jax.shard_map(
        per_device,
        mesh=mesh,
        in_specs=(P(None, "row", None, "col"), P(None, "row", None)),
        out_specs=P(None, "row", "col"),
        check_vma=False,
    )
```

```python
import jax
import jax.numpy as jnp
from jax import lax
from jax.experimental import pallas as pl
from jax.experimental.pallas import tpu as pltpu
from jax.sharding import PartitionSpec as P

F32 = jnp.float32
MESH = pl.DeviceIdType.MESH
BLK = 128
NB = 8
SUPER = 2
NCH = 4
LAG = 3


def lane(x, k):
    return jnp.broadcast_to(x[:, k : k + 1], (8, BLK))


def sub(x, k):
    return jnp.broadcast_to(x[k : k + 1, :], (8, BLK))


def dot_tn(a, b):
    return lax.dot_general(
        a, b, (((0,), (0,)), ((), ())), precision=lax.Precision.HIGHEST, preferred_element_type=F32
    )


def dot_nt(a, b):
    return lax.dot_general(
        a, b, (((1,), (1,)), ((), ())), precision=lax.Precision.HIGHEST, preferred_element_type=F32
    )


def dot_nn(a, b):
    return lax.dot_general(
        a, b, (((1,), (0,)), ((), ())), precision=lax.Precision.HIGHEST, preferred_element_type=F32
    )


def factor_inverse(read, write, poll=None):
    idx = lax.broadcasted_iota(jnp.int32, (8, BLK), 0)
    col = lax.broadcasted_iota(jnp.int32, (8, BLK), 1)
    groups = BLK // 8
    m = [read(i) for i in range(groups)]
    w = [jnp.where(col == idx + 8 * i, 1.0, 0.0).astype(F32) for i in range(groups)]
    u = [None] * groups
    uw = [None] * groups
    for g in range(groups):
        sb = g // SUPER
        near = list(range(g + 1, min(groups, SUPER * (sb + 2))))
        t, v = m[g], w[g]
        piv = [lane(t, 8 * g + k) for k in range(8)]
        low = {i: [lane(m[i], 8 * g + k) for k in range(8)] for i in near}
        rows, rows_w, mult = [], [], {i: [] for i in near}
        for k in range(8):
            scale = lax.rsqrt(sub(piv[k], k))
            mk = jnp.where(idx > k, piv[k] * scale, 0.0)
            rk, rwk = sub(t, k) * scale, sub(v, k) * scale
            rows.append(rk)
            rows_w.append(rwk)
            if k < 7:
                t, v = t - mk * rk, v - mk * rwk
            for i in near:
                mult[i].append(low[i][k] * scale)
            for n in range(k + 1, 8):
                q = sub(piv[n], k) * scale
                piv[n] = piv[n] - mk * q
                for i in near:
                    low[i][n] = low[i][n] - mult[i][k] * q
        ug, uwg = rows[0], rows_w[0]
        for k in range(1, 8):
            ug, uwg = jnp.where(idx == k, rows[k], ug), jnp.where(idx == k, rows_w[k], uwg)
        u[g], uw[g] = ug, uwg
        write(g, uwg)
        for i in near:
            a, b = m[i], w[i]
            for k in range(8):
                a, b = a - mult[i][k] * rows[k], b - mult[i][k] * rows_w[k]
            m[i], w[i] = a, b
        if poll is not None and g % 4 == 3:
            poll(g // 4)
        first = SUPER * (sb + 2)
        if g % SUPER == SUPER - 1 and first < groups:
            us = jnp.concatenate(u[SUPER * sb : g + 1], axis=0)
            ws = jnp.concatenate(uw[SUPER * sb : g + 1], axis=0)
            eu, ew = dot_tn(us, us), dot_tn(us, ws)
            for i in range(first, groups):
                m[i], w[i] = m[i] - eu[8 * i : 8 * i + 8], w[i] - ew[8 * i : 8 * i + 8]


def kernel(
    a_ref, e_hbm, out_ref,
    band, part, rs1, rs2, dpart, drs, cm, winv, wide_inv, stage, outv, ebuf,
    e_sem, ring_s, ring_r, back_s, sib_s, sib_r,
    d_s, d_r, z_s, z_r, g_s, g_r, gs_s, gs_r,
    r1_s, r1_r, r2_s, r2_r, o_s, o_r,
):
    r, c = lax.axis_index("row"), lax.axis_index("col")
    z, q = r // 2, r % 2
    sib = r + 1 - 2 * q
    sf, ss = 1 + 3 * q, 4 - 3 * q
    f, s = (c // sf) % 4, (c // ss) % 4

    def slot(cc):
        return 4 * ((cc // sf) % 4) + (cc // ss) % 4

    def col_of(ff, sx):
        return ff * sf + sx * ss

    def remote(src, dst, send, recv, row, colm):
        return pltpu.make_async_remote_copy(
            src_ref=src, dst_ref=dst, send_sem=send, recv_sem=recv, device_id=(row, colm), device_id_type=MESH
        )

    def wait_bytes(ref, sem):
        pltpu.make_async_copy(ref, ref, sem).wait()

    e_copy = pltpu.make_async_copy(e_hbm.at[:, pl.ds(pl.multiple_of(16 * c, 16), 16), :], ebuf, e_sem)
    e_copy.start()

    barrier = pltpu.get_barrier_semaphore()

    def greet(d, carry):
        pl.semaphore_signal(barrier, inc=1, device_id=(r, (c + d) % 16), device_id_type=MESH)
        return carry

    pl.semaphore_signal(barrier, inc=1, device_id=(sib, c), device_id_type=MESH)
    for d in range(1, 8):
        pl.semaphore_signal(barrier, inc=1, device_id=(2 * ((z + d) % 8) + q, c), device_id_type=MESH)
    lax.fori_loop(1, 16, greet, 0)

    @pl.when(r < 4)
    def _():
        low, high = a_ref[0, 0:256, :], a_ref[1, 0:256, :]
        band[0, r] = low
        band[1, r] = high
        own = dot_nt(low, low) + dot_nt(high, high)
        for t in range(4):

            @pl.when(r == t)
            def _():
                dpart[:, 256 * t : 256 * t + 256] = own

    e_copy.wait()
    pl.semaphore_wait(barrier, 23)

    def chain(h, i):
        pos = z if h == 0 else (9 - z) % 8
        nxt, prv = ((z + 1) % 8, (z + 7) % 8) if h == 0 else ((z + 7) % 8, (z + 1) % 8)
        is_a = (i // NCH + jnp.where(pos == 0, 1, 0)) % 2
        tile = (q + 2 - 2 * is_a) if h == 0 else (q + 2 * is_a)
        k = i % NCH
        n = 2 * NCH * h + NCH * is_a + k
        mine = band.at[h, tile, pl.ds(pl.multiple_of(256 // NCH * k, 256 // NCH), 256 // NCH)]
        fwd = remote(mine, mine, ring_s.at[n], ring_r.at[n], 2 * nxt + q, c)
        back = remote(mine, mine, back_s.at[NCH * h + k], ring_r.at[n], 2 * prv + q, c)
        to_sib = remote(mine, mine, sib_s.at[n], sib_r.at[n], sib, c)
        origin = pos == 1 - is_a
        forwards = jnp.logical_and(pos < 7, pos + is_a > 0)
        returns = jnp.logical_and(pos == 1, is_a == 0)
        return fwd, back, to_sib, origin, forwards, returns

    def ring_step(tick, carry):
        for h in (0, 1):
            pos = z if h == 0 else (9 - z) % 8
            late_by = LAG * jnp.maximum(pos - 1, 0)
            i = jnp.clip(tick - late_by, 0, 2 * NCH - 1)

            @pl.when(jnp.logical_and(tick >= late_by, tick < late_by + 2 * NCH))
            def _():
                fwd, back, to_sib, origin, forwards, returns = chain(h, i)

                @pl.when(jnp.logical_not(origin))
                def _():
                    fwd.wait_recv()

                @pl.when(forwards)
                def _():
                    fwd.start()

                @pl.when(returns)
                def _():
                    back.start()

                to_sib.start()

        return carry

    def ring(first, last):
        lax.fori_loop(first, last, ring_step, 0)

    def from_sibling(second):
        def one(k, carry):
            for h in (0, 1):
                is_a = 1 - second if h == 0 else second
                n = 2 * NCH * h + NCH * is_a + k
                theirs = band.at[h, 1 - q + 2 * second, pl.ds(pl.multiple_of(256 // NCH * k, 256 // NCH), 256 // NCH)]
                remote(theirs, theirs, sib_s.at[n], sib_r.at[n], sib, c).wait_recv()
            return carry

        lax.fori_loop(0, NCH, one, 0)

    def ring_end():
        def one(i, carry):
            for h in (0, 1):
                fwd, back, to_sib, origin, forwards, returns = chain(h, i)

                @pl.when(forwards)
                def _():
                    fwd.wait_send()

                @pl.when(returns)
                def _():
                    back.wait_send()

                to_sib.wait_send()
            return carry

        lax.fori_loop(0, 2 * NCH, one, 0)

        @pl.when(z > 1)
        def _():
            from_sibling(0)

        @pl.when(z != 1)
        def _():
            from_sibling(1)

    def wide(t):
        return pl.ds(0, 256 * (t + 1))

    def at(where, fn, t):
        @pl.when(where)
        def _():
            fn(t)

    def d_start(t):
        def one(d, carry):
            cc = (c + d) % 16
            rows = pl.ds(pl.multiple_of(16 * cc, 16), 16)
            remote(dpart.at[rows, wide(t)], drs.at[d - 1, :, wide(t)], d_s, d_r, r, cc).start()
            return carry

        lax.fori_loop(1, 16, one, 0)

    def d_rest(t):
        for u in range(t):
            dpart[:, 256 * u : 256 * u + 256] = dot_nt(a_ref[0, 0:256, :], band[0, u]) + dot_nt(
                a_ref[1, 0:256, :], band[1, u]
            )
        d_start(t)

    def piece_of(t):
        return cm.at[pl.ds(pl.multiple_of(256 * t + 16 * c, 16), 16), wide(t)]

    def sum_tiles(t):
        width = 256 * (t + 1)
        wait_bytes(drs.at[:, :, wide(t)], d_r)
        total = dpart[pl.ds(pl.multiple_of(16 * c, 16), 16), 0:width]
        for k in range(15):
            total = total + drs[k, :, 0:width]
        piece = piece_of(t)
        piece[...] = ebuf[0, :, 0:width] - total
        for d in range(1, 8):
            remote(piece, piece, z_s, z_r.at[t // 2], 2 * ((z + d) % 8) + q, c).start()

    def gather(t):
        piece = piece_of(t)

        @pl.when(r != t)
        def _():
            remote(piece, piece, z_s, z_r.at[t // 2], sib, c).wait_recv()

        def one(d, carry):
            remote(piece, piece, g_s.at[t // 2], g_r.at[t // 2], r, (c + d) % 16).start()
            return carry

        lax.fori_loop(1, 16, one, 0)

    def share(t):
        wait_bytes(cm.at[pl.ds(0, 240), wide(t)], g_r.at[t // 2])
        rows = cm.at[pl.ds(256 * t, 256), wide(t)]
        remote(rows, rows, gs_s.at[t // 2], gs_r.at[t // 2], sib, c).start()

    def shared(t):
        wait_bytes(cm.at[pl.ds(0, 256), wide(t)], gs_r.at[t // 2])

    def sent(t):
        wait_bytes(cm.at[pl.ds(0, 240), wide(t)], g_s.at[t // 2])
        wait_bytes(cm.at[pl.ds(0, 256), wide(t)], gs_s.at[t // 2])

        @pl.when(r == t)
        def _():
            wait_bytes(drs.at[:, :, wide(t)], d_s)
            wait_bytes(cm.at[pl.ds(0, 112), wide(t)], z_s)

    def product(i, carry):
        n, tl = i // 2, i % 2
        rows = pl.ds(pl.multiple_of(256 * tl, 256), 256)
        res = dot_nt(a_ref[0, rows, :], band[0, n]) + dot_nt(a_ref[1, rows, :], band[1, n])
        for cc in range(16):
            part[slot(cc), n, pl.ds(pl.multiple_of(16 * tl, 16), 16), :] = res[16 * cc : 16 * cc + 16]
        return carry

    def products():
        lax.fori_loop(0, 8, product, 0)
        for d in (1, 2, 3):
            ff = (f + d) % 4
            remote(part.at[pl.ds(4 * ff, 4)], rs1.at[d - 1], r1_s, r1_r, r, col_of(ff, s)).start()

    def sum_first():
        wait_bytes(rs1, r1_r)

        def one(i, carry):
            k, n = i // 4, i % 4
            part[4 * f + k, n] = part[4 * f + k, n] + (rs1[0, k, n] + rs1[1, k, n] + rs1[2, k, n])
            return carry

        lax.fori_loop(0, 16, one, 0)
        for d in (1, 2, 3):
            sx = (s + d) % 4
            remote(part.at[4 * f + sx], rs2.at[d - 1], r2_s, r2_r, r, col_of(f, sx)).start()

    def sum_second():
        wait_bytes(rs2, r2_r)
        for n in range(4):
            total = part[4 * f + s, n] + (rs2[0, n] + rs2[1, n] + rs2[2, n])
            for tl in (0, 1):
                cm[1024 + 16 * tl : 1040 + 16 * tl, 256 * n : 256 * n + 256] = (
                    ebuf[tl, :, 256 * n : 256 * n + 256] - total[16 * tl : 16 * tl + 16]
                )

    def rows_solved(top, bottom, p, end):
        left, below = 256 * p, 256 * (p + 1)
        x = dot_nt(cm[top:bottom, left:below], wide_inv[p])
        cm[top:bottom, left:below] = x
        if below < end:
            cm[top:bottom, below:end] = cm[top:bottom, below:end] - dot_nt(x, cm[below:end, left:below])

    def pair_inverse(p):
        w0, w1 = winv[2 * p], winv[2 * p + 1]
        mid = dot_nn(cm[256 * p + 128 : 256 * p + 256, 256 * p : 256 * p + 128], w0)
        wide_inv[p, 0:128, 0:128] = w0
        wide_inv[p, 0:128, 128:256] = jnp.zeros((128, 128), F32)
        wide_inv[p, 128:256, 0:128] = -dot_nn(w1, mid)
        wide_inv[p, 128:256, 128:256] = w1

    def before_pair(t):
        top = 256 * t
        for p in range(t):
            rows_solved(top, top + 256, p, top)
        x = cm[top : top + 256, 0:top]
        cm[top : top + 256, top : top + 256] = cm[top : top + 256, top : top + 256] - dot_nt(x, x)

    def after_block(n):
        if n % 2 == 0:
            top, left = BLK * (n + 1), BLK * n
            x = dot_nt(cm[top : top + BLK, left:top], winv[n])
            cm[top : top + BLK, left:top] = x
            cm[top : top + BLK, top : top + BLK] = cm[top : top + BLK, top : top + BLK] - dot_nt(x, x)
        elif n < NB - 1:
            pair_inverse(n // 2)

    def own_rows_solved():
        for p in range(3):
            rows_solved(1024, 1056, p, 1024)
        x = dot_nt(cm[1024:1056, 768:896], winv[6])
        cm[1024:1056, 768:896] = x
        cm[1024:1056, 896:1024] = cm[1024:1056, 896:1024] - dot_nt(x, cm[896:1024, 768:896])

    step = lax.broadcasted_iota(jnp.int32, (16, 64), 0)
    lanes = lax.broadcasted_iota(jnp.int32, (16, 64), 1)
    my_rows = pl.ds(pl.multiple_of(16 * c, 16), 16)

    def out_send(d):
        cc = (c + d) % 16
        return remote(stage.at[cc], outv.at[:, my_rows], o_s.at[d - 1], o_r.at[d - 1], r, cc)

    def out_start(first, last):
        for tl in (0, 1):
            g0 = (16 * tl + r) * 256 + 16 * c
            for cc in range(first, last):
                x = cm[1024 + 16 * tl : 1040 + 16 * tl, 64 * cc : 64 * cc + 64]
                stage[cc, tl] = jnp.where(lanes + 64 * cc <= step + g0, x, 0.0)

        def one(cc, carry):
            @pl.when(cc != c)
            def _():
                out_send((cc - c + 16) % 16).start()

            return carry

        lax.fori_loop(first, last, one, 0)

    @pl.when(r == 0)
    def _():
        d_start(0)

    ring(0, 4)

    @pl.when(z == 0)
    def _():
        from_sibling(0)

        @pl.when(r == 1)
        def _():
            d_rest(1)

    at(r == 0, sum_tiles, 0)
    ring(4, 6)
    at(q == 0, gather, 0)
    at(r == 1, sum_tiles, 1)
    ring(6, 8)
    at(q == 0, share, 0)

    @pl.when(z == 1)
    def _():
        from_sibling(0)
        from_sibling(1)

    at(r == 2, d_rest, 2)
    at(r == 3, d_rest, 3)
    at(q == 1, gather, 1)
    ring(8, 10)
    at(q == 1, shared, 0)
    at(q == 0, sent, 0)

    def before(n):
        if n == 2:
            at(q == 0, shared, 1)
            at(q == 1, sent, 1)
            at(q == 0, gather, 2)
            at(q == 1, gather, 3)
        if n == 4:
            at(q == 1, shared, 2)
            at(q == 0, sent, 2)
        if n == 6:
            at(q == 0, shared, 3)
            at(q == 1, sent, 3)
        before_pair(n // 2)

    def after(n):
        after_block(n)
        if n == 0:
            at(q == 1, share, 1)
            at(r == 2, sum_tiles, 2)
            at(r == 3, sum_tiles, 3)
        if n == 2:
            at(q == 0, share, 2)
            at(q == 1, share, 3)
        if n == 3:
            ring_end()
            products()
        if n == 5:
            sum_first()
        if n == 6:
            sum_second()
            own_rows_solved()
            out_start(0, 14)

    def block(j, carry):
        for n in (2, 4, 6):

            @pl.when(j == n)
            def _():
                before(n)

        cols = pl.ds(pl.multiple_of(BLK * j, BLK), BLK)

        def read(i):
            return cm[pl.ds(pl.multiple_of(BLK * j + 8 * i, 8), 8), cols]

        def write(g, x):
            winv[j, 8 * g : 8 * g + 8, :] = x

        def poll(k):
            ring(10 + 4 * j + k, 11 + 4 * j + k)

        factor_inverse(read, write, poll)
        for n in range(NB):

            @pl.when(j == n)
            def _():
                after(n)

        return carry

    lax.fori_loop(0, NB, block, 0)
    cm[1024:1056, 896:1024] = dot_nt(cm[1024:1056, 896:1024], winv[7])
    out_start(14, 16)
    outv[:, my_rows] = stage[c]

    wait_bytes(rs1, r1_s)
    wait_bytes(rs2, r2_s)

    def out_end(d, carry):
        copy = out_send(d)
        copy.wait_send()
        copy.wait_recv()
        return carry

    lax.fori_loop(1, 16, out_end, 0)
    out_ref[...] = outv[...]


def per_device(old_factor, panel_block):
    a = jnp.transpose(old_factor, (2, 0, 1, 3)).reshape(2, 512, 256)
    dma = pltpu.SemaphoreType.DMA
    scratch = [
        pltpu.VMEM((2, 4, 256, 256), F32),
        pltpu.VMEM((16, 4, 32, 256), F32),
        pltpu.VMEM((3, 4, 4, 32, 256), F32),
        pltpu.VMEM((3, 4, 32, 256), F32),
        pltpu.VMEM((256, 1024), F32),
        pltpu.VMEM((15, 16, 1024), F32),
        pltpu.VMEM((1056, 1024), F32),
        pltpu.VMEM((NB, BLK, BLK), F32),
        pltpu.VMEM((3, 256, 256), F32),
        pltpu.VMEM((16, 2, 16, 64), F32),
        pltpu.VMEM((2, 256, 64), F32),
        pltpu.VMEM((2, 16, 1024), F32),
        dma, dma((4 * NCH,)), dma((4 * NCH,)), dma((2 * NCH,)), dma((4 * NCH,)), dma((4 * NCH,)),
        dma, dma, dma, dma((2,)), dma((2,)), dma((2,)), dma((2,)), dma((2,)),
        dma, dma, dma, dma, dma((15,)), dma((15,)),
    ]
    return pl.pallas_call(
        kernel,
        out_shape=jax.ShapeDtypeStruct((2, 256, 64), F32),
        in_specs=[pl.BlockSpec(memory_space=pltpu.VMEM), pl.BlockSpec(memory_space=pl.ANY)],
        out_specs=pl.BlockSpec(memory_space=pltpu.VMEM),
        scratch_shapes=scratch,
        compiler_params=pltpu.CompilerParams(
            collective_id=0, has_side_effects=True, vmem_limit_bytes=60 * 1024 * 1024
        ),
    )(a, panel_block)


def solution(mesh):
    return jax.shard_map(
        per_device,
        mesh=mesh,
        in_specs=(P(None, "row", None, "col"), P(None, "row", None)),
        out_specs=P(None, "row", "col"),
        check_vma=False,
    )
```

```python
import jax
import jax.numpy as jnp
from jax import lax
from jax.experimental import pallas as pl
from jax.experimental.pallas import tpu as pltpu
from jax.sharding import PartitionSpec as P

F32 = jnp.float32
MESH = pl.DeviceIdType.MESH
BLK = 128
NB = 8
SUPER = 2
NCH = 4
LAG = 3


def lane(x, k):
    return jnp.broadcast_to(x[:, k : k + 1], (8, BLK))


def sub(x, k):
    return jnp.broadcast_to(x[k : k + 1, :], (8, BLK))


def dot_tn(a, b):
    return lax.dot_general(
        a, b, (((0,), (0,)), ((), ())), precision=lax.Precision.HIGHEST, preferred_element_type=F32
    )


def dot_nt(a, b):
    return lax.dot_general(
        a, b, (((1,), (1,)), ((), ())), precision=lax.Precision.HIGHEST, preferred_element_type=F32
    )


def factor_inverse(read, write, poll=None):
    idx = lax.broadcasted_iota(jnp.int32, (8, BLK), 0)
    col = lax.broadcasted_iota(jnp.int32, (8, BLK), 1)
    groups = BLK // 8
    m = [read(i) for i in range(groups)]
    w = [jnp.where(col == idx + 8 * i, 1.0, 0.0).astype(F32) for i in range(groups)]
    u = [None] * groups
    uw = [None] * groups
    for g in range(groups):
        sb = g // SUPER
        near = list(range(g + 1, min(groups, SUPER * (sb + 2))))
        t, v = m[g], w[g]
        piv = [lane(t, 8 * g + k) for k in range(8)]
        low = {i: [lane(m[i], 8 * g + k) for k in range(8)] for i in near}
        rows, rows_w, mult = [], [], {i: [] for i in near}
        for k in range(8):
            scale = lax.rsqrt(sub(piv[k], k))
            mk = jnp.where(idx > k, piv[k] * scale, 0.0)
            rk, rwk = sub(t, k) * scale, sub(v, k) * scale
            rows.append(rk)
            rows_w.append(rwk)
            if k < 7:
                t, v = t - mk * rk, v - mk * rwk
            for i in near:
                mult[i].append(low[i][k] * scale)
            for n in range(k + 1, 8):
                q = sub(piv[n], k) * scale
                piv[n] = piv[n] - mk * q
                for i in near:
                    low[i][n] = low[i][n] - mult[i][k] * q
        ug, uwg = rows[0], rows_w[0]
        for k in range(1, 8):
            ug, uwg = jnp.where(idx == k, rows[k], ug), jnp.where(idx == k, rows_w[k], uwg)
        u[g], uw[g] = ug, uwg
        write(g, uwg)
        for i in near:
            a, b = m[i], w[i]
            for k in range(8):
                a, b = a - mult[i][k] * rows[k], b - mult[i][k] * rows_w[k]
            m[i], w[i] = a, b
        if poll is not None and g % 4 == 3:
            poll(g // 4)
        first = SUPER * (sb + 2)
        if g % SUPER == SUPER - 1 and first < groups:
            us = jnp.concatenate(u[SUPER * sb : g + 1], axis=0)
            ws = jnp.concatenate(uw[SUPER * sb : g + 1], axis=0)
            eu, ew = dot_tn(us, us), dot_tn(us, ws)
            for i in range(first, groups):
                m[i], w[i] = m[i] - eu[8 * i : 8 * i + 8], w[i] - ew[8 * i : 8 * i + 8]


def kernel(
    a_ref, e_hbm, out_ref,
    band, part, rs1, rs2, dpart, drs, cm, winv, stage, outv, ebuf,
    e_sem, ring_s, ring_r, back_s, sib_s, sib_r,
    d_s, d_r, z_s, z_r, g_s, g_r, gs_s, gs_r,
    r1_s, r1_r, r2_s, r2_r, o_s, o_r,
):
    r, c = lax.axis_index("row"), lax.axis_index("col")
    z, q = r // 2, r % 2
    sib = r + 1 - 2 * q
    sf, ss = 1 + 3 * q, 4 - 3 * q
    f, s = (c // sf) % 4, (c // ss) % 4

    def slot(cc):
        return 4 * ((cc // sf) % 4) + (cc // ss) % 4

    def col_of(ff, sx):
        return ff * sf + sx * ss

    def remote(src, dst, send, recv, row, colm):
        return pltpu.make_async_remote_copy(
            src_ref=src, dst_ref=dst, send_sem=send, recv_sem=recv, device_id=(row, colm), device_id_type=MESH
        )

    def wait_bytes(ref, sem):
        pltpu.make_async_copy(ref, ref, sem).wait()

    e_copy = pltpu.make_async_copy(e_hbm.at[:, pl.ds(pl.multiple_of(16 * c, 16), 16), :], ebuf, e_sem)
    e_copy.start()

    barrier = pltpu.get_barrier_semaphore()

    def greet(d, carry):
        pl.semaphore_signal(barrier, inc=1, device_id=(r, (c + d) % 16), device_id_type=MESH)
        return carry

    pl.semaphore_signal(barrier, inc=1, device_id=(sib, c), device_id_type=MESH)
    for d in range(1, 8):
        pl.semaphore_signal(barrier, inc=1, device_id=(2 * ((z + d) % 8) + q, c), device_id_type=MESH)
    lax.fori_loop(1, 16, greet, 0)

    @pl.when(r < 4)
    def _():
        low, high = a_ref[0, 0:256, :], a_ref[1, 0:256, :]
        band[0, r] = low
        band[1, r] = high
        dpart[r] = dot_nt(low, low) + dot_nt(high, high)

    e_copy.wait()
    pl.semaphore_wait(barrier, 23)

    def chain(h, i):
        pos = z if h == 0 else (9 - z) % 8
        nxt, prv = ((z + 1) % 8, (z + 7) % 8) if h == 0 else ((z + 7) % 8, (z + 1) % 8)
        is_a = (i // NCH + jnp.where(pos == 0, 1, 0)) % 2
        tile = (q + 2 - 2 * is_a) if h == 0 else (q + 2 * is_a)
        k = i % NCH
        n = 2 * NCH * h + NCH * is_a + k
        mine = band.at[h, tile, pl.ds(pl.multiple_of(256 // NCH * k, 256 // NCH), 256 // NCH)]
        fwd = remote(mine, mine, ring_s.at[n], ring_r.at[n], 2 * nxt + q, c)
        back = remote(mine, mine, back_s.at[NCH * h + k], ring_r.at[n], 2 * prv + q, c)
        to_sib = remote(mine, mine, sib_s.at[n], sib_r.at[n], sib, c)
        origin = pos == 1 - is_a
        forwards = jnp.logical_and(pos < 7, pos + is_a > 0)
        returns = jnp.logical_and(pos == 1, is_a == 0)
        return fwd, back, to_sib, origin, forwards, returns

    def ring_step(tick, carry):
        for h in (0, 1):
            pos = z if h == 0 else (9 - z) % 8
            late_by = LAG * jnp.maximum(pos - 1, 0)
            i = jnp.clip(tick - late_by, 0, 2 * NCH - 1)

            @pl.when(jnp.logical_and(tick >= late_by, tick < late_by + 2 * NCH))
            def _():
                fwd, back, to_sib, origin, forwards, returns = chain(h, i)

                @pl.when(jnp.logical_not(origin))
                def _():
                    fwd.wait_recv()

                @pl.when(forwards)
                def _():
                    fwd.start()

                @pl.when(returns)
                def _():
                    back.start()

                to_sib.start()

        return carry

    def ring(first, last):
        lax.fori_loop(first, last, ring_step, 0)

    def from_sibling(second):
        def one(k, carry):
            for h in (0, 1):
                is_a = 1 - second if h == 0 else second
                n = 2 * NCH * h + NCH * is_a + k
                theirs = band.at[h, 1 - q + 2 * second, pl.ds(pl.multiple_of(256 // NCH * k, 256 // NCH), 256 // NCH)]
                remote(theirs, theirs, sib_s.at[n], sib_r.at[n], sib, c).wait_recv()
            return carry

        lax.fori_loop(0, NCH, one, 0)

    def ring_end():
        def one(i, carry):
            for h in (0, 1):
                fwd, back, to_sib, origin, forwards, returns = chain(h, i)

                @pl.when(forwards)
                def _():
                    fwd.wait_send()

                @pl.when(returns)
                def _():
                    back.wait_send()

                to_sib.wait_send()
            return carry

        lax.fori_loop(0, 2 * NCH, one, 0)

        @pl.when(z > 1)
        def _():
            from_sibling(0)

        @pl.when(z != 1)
        def _():
            from_sibling(1)

    def d_send(u, d):
        cc = (c + d) % 16
        rows = pl.ds(pl.multiple_of(16 * cc, 16), 16)
        return remote(dpart.at[u, rows], drs.at[u, d - 1], d_s.at[u], d_r.at[u], r, cc)

    def d_start(u):
        def one(d, carry):
            d_send(u, d).start()
            return carry

        lax.fori_loop(1, 16, one, 0)

    def d_rest(owner):
        @pl.when(r == owner)
        def _():
            for u in range(owner):
                dpart[u] = dot_nt(a_ref[0, 0:256, :], band[0, u]) + dot_nt(a_ref[1, 0:256, :], band[1, u])
                d_start(u)

    def piece_of(t, u):
        rows = pl.ds(pl.multiple_of(256 * t + 16 * c, 16), 16)
        return cm.at[rows, pl.ds(256 * u, 256)]

    def tile_of(t, u):
        return cm.at[pl.ds(pl.multiple_of(256 * t, 256), 256), pl.ds(256 * u, 256)]

    def rows_of(n):
        return cm.at[pl.ds(0, n), pl.ds(0, 256)]

    def sum_tiles(tt):
        for u in range(2 * tt + 2):

            @pl.when(jnp.logical_and(z == tt, u <= r))
            def _():
                wait_bytes(drs.at[u], d_r.at[u])
                total = dpart[u, pl.ds(pl.multiple_of(16 * c, 16), 16), :]
                for k in range(15):
                    total = total + drs[u, k]
                piece = piece_of(r, u)
                piece[...] = ebuf[0, :, 256 * u : 256 * u + 256] - total

                def one(d, carry):
                    remote(piece, piece, z_s.at[u], z_r.at[tt, u], 2 * ((z + d) % 8) + q, c).start()
                    return carry

                lax.fori_loop(1, 8, one, 0)

    def tiles(tt, fn):
        for u in range(2 * tt + 2):
            t = 2 * tt + q

            @pl.when(u <= t)
            def _():
                fn(tt, t, u)

    def gather(tt, t, u):
        piece = piece_of(t, u)

        @pl.when(r != t)
        def _():
            remote(piece, piece, z_s.at[u], z_r.at[tt, u], sib, c).wait_recv()

        def one(d, carry):
            remote(piece, piece, g_s.at[tt, u], g_r.at[tt, u], r, (c + d) % 16).start()
            return carry

        lax.fori_loop(1, 16, one, 0)

    def share(tt, t, u):
        wait_bytes(rows_of(240), g_r.at[tt, u])
        tile = tile_of(t, u)
        remote(tile, tile, gs_s.at[tt, u], gs_r.at[tt, u], sib, c).start()

    def shared(tt):
        for u in range(2 * tt + 2):
            t = 2 * tt + 1 - q

            @pl.when(u <= t)
            def _():
                wait_bytes(rows_of(256), gs_r.at[tt, u])

    def sent(tt):
        def one(tt, t, u):
            wait_bytes(rows_of(240), g_s.at[tt, u])
            wait_bytes(rows_of(256), gs_s.at[tt, u])

        tiles(tt, one)
        for u in range(2 * tt + 2):

            @pl.when(jnp.logical_and(z == tt, u <= r))
            def _():
                wait_bytes(drs.at[u], d_s.at[u])
                wait_bytes(rows_of(112), z_s.at[u])

    def product(i, carry):
        n, tl = i // 2, i % 2
        rows = pl.ds(pl.multiple_of(256 * tl, 256), 256)
        known = jnp.logical_and(r < 4, tl == 0)

        @pl.when(jnp.logical_and(known, n <= r))
        def _():
            for cc in range(16):
                part[slot(cc), n, 0:16, :] = dpart[n, 16 * cc : 16 * cc + 16, :]

        @pl.when(jnp.logical_and(known, n > r))
        def _():
            for cc in range(16):
                part[cc, n, 0:16, :] = jnp.zeros((16, 256), F32)

        @pl.when(jnp.logical_not(known))
        def _():
            res = dot_nt(a_ref[0, rows, :], band[0, n]) + dot_nt(a_ref[1, rows, :], band[1, n])
            for cc in range(16):
                part[slot(cc), n, pl.ds(pl.multiple_of(16 * tl, 16), 16), :] = res[16 * cc : 16 * cc + 16]

        return carry

    def products():
        lax.fori_loop(0, 8, product, 0)
        for d in (1, 2, 3):
            ff = (f + d) % 4
            remote(part.at[pl.ds(4 * ff, 4)], rs1.at[d - 1], r1_s, r1_r, r, col_of(ff, s)).start()

    def sum_first():
        wait_bytes(rs1, r1_r)

        def one(i, carry):
            k, n = i // 4, i % 4
            part[4 * f + k, n] = part[4 * f + k, n] + (rs1[0, k, n] + rs1[1, k, n] + rs1[2, k, n])
            return carry

        lax.fori_loop(0, 16, one, 0)
        for d in (1, 2, 3):
            sx = (s + d) % 4
            remote(part.at[4 * f + sx], rs2.at[d - 1], r2_s, r2_r, r, col_of(f, sx)).start()

    def sum_second():
        wait_bytes(rs2, r2_r)
        for n in range(4):
            total = part[4 * f + s, n] + (rs2[0, n] + rs2[1, n] + rs2[2, n])
            for tl in (0, 1):
                cm[1024 + 16 * tl : 1040 + 16 * tl, 256 * n : 256 * n + 256] = (
                    ebuf[tl, :, 256 * n : 256 * n + 256] - total[16 * tl : 16 * tl + 16]
                )

    def solve_rows(j):
        x = dot_nt(cm[1024:1056, BLK * j : BLK * j + BLK], winv[j])
        cm[1024:1056, BLK * j : BLK * j + BLK] = x
        if j < NB - 1:
            below = BLK * (j + 1)
            cm[1024:1056, below:1024] = cm[1024:1056, below:1024] - dot_nt(x, cm[below:1024, BLK * j : BLK * j + BLK])

    def blocks(first, last, bottom, rows_from, ticks, after):
        def block(j, carry):
            cols = pl.ds(pl.multiple_of(BLK * j, BLK), BLK)

            def read(i):
                return cm[pl.ds(pl.multiple_of(BLK * j + 8 * i, 8), 8), cols]

            def write(g, x):
                winv[j, 8 * g : 8 * g + 8, :] = x

            def poll(n):
                ring(ticks + 4 * j + n, ticks + 4 * j + n + 1)

            factor_inverse(read, write, poll if ticks else None)
            for n in range(first, last):

                @pl.when(j == n)
                def _():
                    if n == rows_from:
                        for k in range(n):
                            solve_rows(k)
                    top, end = BLK * (n + 1), (1056 if n >= rows_from else bottom)
                    if top < end:
                        x = dot_nt(cm[top:end, BLK * n : BLK * n + BLK], winv[n])
                        cm[top:end, BLK * n : BLK * n + BLK] = x
                        for kb in range(top, bottom, 256):
                            width = min(256, bottom - kb)
                            cm[kb:end, kb : kb + width] = cm[kb:end, kb : kb + width] - dot_nt(
                                x[kb - top :], x[kb - top : kb - top + width]
                            )
                    after(n)

            return carry

        lax.fori_loop(first, last, block, 0)

    @pl.when(r < 4)
    def _():
        d_start(r)

    ring(0, 4)

    @pl.when(z == 0)
    def _():
        from_sibling(0)

    d_rest(1)
    ring(4, 7)
    sum_tiles(0)
    ring(7, 10)
    tiles(0, gather)

    @pl.when(z == 1)
    def _():
        from_sibling(0)
        from_sibling(1)

    d_rest(2)
    d_rest(3)
    ring(10, 12)
    tiles(0, share)
    ring(12, 14)
    sum_tiles(1)
    shared(0)
    sent(0)

    def after_first(n):
        if n == 0:
            tiles(1, gather)
        if n == 2:
            ring_end()
            products()
            tiles(1, share)
        if n == 3:
            shared(1)
            sent(1)

    blocks(0, 4, 512, NB, 14, after_first)

    for k in range(4):
        x = dot_nt(cm[512:1024, BLK * k : BLK * k + BLK], winv[k])
        cm[512:1024, BLK * k : BLK * k + BLK] = x
        if k < 3:
            below = BLK * (k + 1)
            cm[512:1024, below:512] = cm[512:1024, below:512] - dot_nt(x, cm[below:512, BLK * k : BLK * k + BLK])
    for kb in (512, 768):
        cm[kb:1024, kb : kb + 256] = cm[kb:1024, kb : kb + 256] - dot_nt(cm[kb:1024, 0:512], cm[kb : kb + 256, 0:512])

    step = lax.broadcasted_iota(jnp.int32, (16, 64), 0)
    lanes = lax.broadcasted_iota(jnp.int32, (16, 64), 1)
    my_rows = pl.ds(pl.multiple_of(16 * c, 16), 16)

    def out_send(d):
        cc = (c + d) % 16
        return remote(stage.at[cc], outv.at[:, my_rows], o_s.at[d - 1], o_r.at[d - 1], r, cc)

    def out_start(first, last):
        for tl in (0, 1):
            g0 = (16 * tl + r) * 256 + 16 * c
            for cc in range(first, last):
                x = cm[1024 + 16 * tl : 1040 + 16 * tl, 64 * cc : 64 * cc + 64]
                stage[cc, tl] = jnp.where(lanes + 64 * cc <= step + g0, x, 0.0)

        def one(cc, carry):
            @pl.when(cc != c)
            def _():
                out_send((cc - c + 16) % 16).start()

            return carry

        lax.fori_loop(first, last, one, 0)

    def after_second(n):
        if n == 4:
            sum_first()
        if n == 5:
            sum_second()
        if n == 6:
            out_start(0, 14)

    blocks(4, 8, 1024, 6, 0, after_second)
    out_start(14, 16)
    outv[:, my_rows] = stage[c]

    wait_bytes(rs1, r1_s)
    wait_bytes(rs2, r2_s)

    def out_end(d, carry):
        copy = out_send(d)
        copy.wait_send()
        copy.wait_recv()
        return carry

    lax.fori_loop(1, 16, out_end, 0)
    for tl in (0, 1):
        out_ref[tl] = outv[tl].T


def per_device(old_factor, panel_block):
    a = jnp.transpose(old_factor, (2, 0, 1, 3)).reshape(2, 512, 256)
    dma = pltpu.SemaphoreType.DMA
    scratch = [
        pltpu.VMEM((2, 4, 256, 256), F32),
        pltpu.VMEM((16, 4, 32, 256), F32),
        pltpu.VMEM((3, 4, 4, 32, 256), F32),
        pltpu.VMEM((3, 4, 32, 256), F32),
        pltpu.VMEM((4, 256, 256), F32),
        pltpu.VMEM((4, 15, 16, 256), F32),
        pltpu.VMEM((1056, 1024), F32),
        pltpu.VMEM((NB, BLK, BLK), F32),
        pltpu.VMEM((16, 2, 16, 64), F32),
        pltpu.VMEM((2, 256, 64), F32),
        pltpu.VMEM((2, 16, 1024), F32),
        dma, dma((4 * NCH,)), dma((4 * NCH,)), dma((2 * NCH,)), dma((4 * NCH,)), dma((4 * NCH,)),
        dma((4,)), dma((4,)), dma((4,)), dma((2, 4)), dma((2, 4)), dma((2, 4)), dma((2, 4)), dma((2, 4)),
        dma, dma, dma, dma, dma((15,)), dma((15,)),
    ]
    out = pl.pallas_call(
        kernel,
        out_shape=jax.ShapeDtypeStruct((2, 64, 256), F32),
        in_specs=[pl.BlockSpec(memory_space=pltpu.VMEM), pl.BlockSpec(memory_space=pl.ANY)],
        out_specs=pl.BlockSpec(memory_space=pltpu.VMEM),
        scratch_shapes=scratch,
        compiler_params=pltpu.CompilerParams(
            collective_id=0, has_side_effects=True, vmem_limit_bytes=62 * 1024 * 1024
        ),
    )(a, panel_block)
    return jnp.transpose(out, (0, 2, 1))


def solution(mesh):
    return jax.shard_map(
        per_device,
        mesh=mesh,
        in_specs=(P(None, "row", None, "col"), P(None, "row", None)),
        out_specs=P(None, "row", "col"),
        check_vma=False,
    )
```

```python
import jax
import jax.numpy as jnp
from jax import lax
from jax.experimental import pallas as pl
from jax.experimental.pallas import tpu as pltpu
from jax.sharding import PartitionSpec as P

F32 = jnp.float32
MESH = pl.DeviceIdType.MESH
BLK = 128
NB = 8
SUPER = 2
NCH = 4
LAG = 3


def lane(x, k):
    return jnp.broadcast_to(x[:, k : k + 1], (8, BLK))


def sub(x, k):
    return jnp.broadcast_to(x[k : k + 1, :], (8, BLK))


def dot_tn(a, b):
    return lax.dot_general(
        a, b, (((0,), (0,)), ((), ())), precision=lax.Precision.HIGHEST, preferred_element_type=F32
    )


def dot_nt(a, b):
    return lax.dot_general(
        a, b, (((1,), (1,)), ((), ())), precision=lax.Precision.HIGHEST, preferred_element_type=F32
    )


def factor_inverse(read, write, poll=None):
    idx = lax.broadcasted_iota(jnp.int32, (8, BLK), 0)
    col = lax.broadcasted_iota(jnp.int32, (8, BLK), 1)
    groups = BLK // 8
    m = [read(i) for i in range(groups)]
    w = [jnp.where(col == idx + 8 * i, 1.0, 0.0).astype(F32) for i in range(groups)]
    u = [None] * groups
    uw = [None] * groups
    for g in range(groups):
        sb = g // SUPER
        near = list(range(g + 1, min(groups, SUPER * (sb + 2))))
        t, v = m[g], w[g]
        piv = ahead if g else [lane(t, 8 * g + k) for k in range(8)]
        ahead = [lane(m[g + 1], 8 * g + 8 + k) for k in range(8)] if g < groups - 1 else None
        low = {i: [lane(m[i], 8 * g + k) for k in range(8)] for i in near}
        rows, rows_w, mult = [], [], {i: [] for i in near}
        for k in range(8):
            scale = lax.rsqrt(sub(piv[k], k))
            mk = jnp.where(idx > k, piv[k] * scale, 0.0)
            rk, rwk = sub(t, k) * scale, sub(v, k) * scale
            rows.append(rk)
            rows_w.append(rwk)
            if k < 7:
                t, v = t - mk * rk, v - mk * rwk
            for i in near:
                mult[i].append(low[i][k] * scale)
            if ahead is not None:
                lk = mult[g + 1][k]
                ahead = [ahead[n] - lk * sub(lk, n) for n in range(8)]
            for n in range(k + 1, 8):
                q = sub(piv[n], k) * scale
                piv[n] = piv[n] - mk * q
                for i in near:
                    low[i][n] = low[i][n] - mult[i][k] * q
        ug, uwg = rows[0], rows_w[0]
        for k in range(1, 8):
            ug, uwg = jnp.where(idx == k, rows[k], ug), jnp.where(idx == k, rows_w[k], uwg)
        u[g], uw[g] = ug, uwg
        write(g, uwg)
        for i in near:
            a, b = m[i], w[i]
            for k in range(8):
                a, b = a - mult[i][k] * rows[k], b - mult[i][k] * rows_w[k]
            m[i], w[i] = a, b
        if poll is not None and g % 4 == 3:
            poll(g // 4)
        first = SUPER * (sb + 2)
        if g % SUPER == SUPER - 1 and first < groups:
            us = jnp.concatenate(u[SUPER * sb : g + 1], axis=0)
            ws = jnp.concatenate(uw[SUPER * sb : g + 1], axis=0)
            eu, ew = dot_tn(us, us), dot_tn(us, ws)
            for i in range(first, groups):
                m[i], w[i] = m[i] - eu[8 * i : 8 * i + 8], w[i] - ew[8 * i : 8 * i + 8]


def kernel(
    a_ref, e_hbm, out_ref,
    band, part, rs1, rs2, dpart, drs, cm, winv, stage, outv, ebuf,
    e_sem, ring_s, ring_r, back_s, sib_s, sib_r,
    d_s, d_r, z_s, z_r, g_s, g_r, gs_s, gs_r,
    r1_s, r1_r, r2_s, r2_r, o_s, o_r,
):
    r, c = lax.axis_index("row"), lax.axis_index("col")
    z, q = r // 2, r % 2
    sib = r + 1 - 2 * q
    sf, ss = 1 + 3 * q, 4 - 3 * q
    f, s = (c // sf) % 4, (c // ss) % 4

    def slot(cc):
        return 4 * ((cc // sf) % 4) + (cc // ss) % 4

    def col_of(ff, sx):
        return ff * sf + sx * ss

    def remote(src, dst, send, recv, row, colm):
        return pltpu.make_async_remote_copy(
            src_ref=src, dst_ref=dst, send_sem=send, recv_sem=recv, device_id=(row, colm), device_id_type=MESH
        )

    def wait_bytes(ref, sem):
        pltpu.make_async_copy(ref, ref, sem).wait()

    e_copy = pltpu.make_async_copy(e_hbm.at[:, pl.ds(pl.multiple_of(16 * c, 16), 16), :], ebuf, e_sem)
    e_copy.start()

    barrier = pltpu.get_barrier_semaphore()

    def greet(d, carry):
        pl.semaphore_signal(barrier, inc=1, device_id=(r, (c + d) % 16), device_id_type=MESH)
        return carry

    pl.semaphore_signal(barrier, inc=1, device_id=(sib, c), device_id_type=MESH)
    for d in range(1, 8):
        pl.semaphore_signal(barrier, inc=1, device_id=(2 * ((z + d) % 8) + q, c), device_id_type=MESH)
    lax.fori_loop(1, 16, greet, 0)

    @pl.when(r < 4)
    def _():
        low, high = a_ref[0, 0:256, :], a_ref[1, 0:256, :]
        band[0, r] = low
        band[1, r] = high
        dpart[r] = dot_nt(low, low) + dot_nt(high, high)

    e_copy.wait()
    pl.semaphore_wait(barrier, 23)

    def chain(h, i):
        pos = z if h == 0 else (9 - z) % 8
        nxt, prv = ((z + 1) % 8, (z + 7) % 8) if h == 0 else ((z + 7) % 8, (z + 1) % 8)
        is_a = (i // NCH + jnp.where(pos == 0, 1, 0)) % 2
        tile = (q + 2 - 2 * is_a) if h == 0 else (q + 2 * is_a)
        k = i % NCH
        n = 2 * NCH * h + NCH * is_a + k
        mine = band.at[h, tile, pl.ds(pl.multiple_of(256 // NCH * k, 256 // NCH), 256 // NCH)]
        fwd = remote(mine, mine, ring_s.at[n], ring_r.at[n], 2 * nxt + q, c)
        back = remote(mine, mine, back_s.at[NCH * h + k], ring_r.at[n], 2 * prv + q, c)
        to_sib = remote(mine, mine, sib_s.at[n], sib_r.at[n], sib, c)
        origin = pos == 1 - is_a
        forwards = jnp.logical_and(pos < 7, pos + is_a > 0)
        returns = jnp.logical_and(pos == 1, is_a == 0)
        return fwd, back, to_sib, origin, forwards, returns

    def ring_step(tick, carry):
        for h in (0, 1):
            pos = z if h == 0 else (9 - z) % 8
            late_by = LAG * jnp.maximum(pos - 1, 0)
            i = jnp.clip(tick - late_by, 0, 2 * NCH - 1)

            @pl.when(jnp.logical_and(tick >= late_by, tick < late_by + 2 * NCH))
            def _():
                fwd, back, to_sib, origin, forwards, returns = chain(h, i)

                @pl.when(jnp.logical_not(origin))
                def _():
                    fwd.wait_recv()

                @pl.when(forwards)
                def _():
                    fwd.start()

                @pl.when(returns)
                def _():
                    back.start()

                to_sib.start()

        return carry

    def ring(first, last):
        lax.fori_loop(first, last, ring_step, 0)

    def from_sibling(second):
        def one(k, carry):
            for h in (0, 1):
                is_a = 1 - second if h == 0 else second
                n = 2 * NCH * h + NCH * is_a + k
                theirs = band.at[h, 1 - q + 2 * second, pl.ds(pl.multiple_of(256 // NCH * k, 256 // NCH), 256 // NCH)]
                remote(theirs, theirs, sib_s.at[n], sib_r.at[n], sib, c).wait_recv()
            return carry

        lax.fori_loop(0, NCH, one, 0)

    def ring_end():
        def one(i, carry):
            for h in (0, 1):
                fwd, back, to_sib, origin, forwards, returns = chain(h, i)

                @pl.when(forwards)
                def _():
                    fwd.wait_send()

                @pl.when(returns)
                def _():
                    back.wait_send()

                to_sib.wait_send()
            return carry

        lax.fori_loop(0, 2 * NCH, one, 0)

        @pl.when(z > 1)
        def _():
            from_sibling(0)

        @pl.when(z != 1)
        def _():
            from_sibling(1)

    def d_send(u, d):
        cc = (c + d) % 16
        rows = pl.ds(pl.multiple_of(16 * cc, 16), 16)
        return remote(dpart.at[u, rows], drs.at[u, d - 1], d_s.at[u], d_r.at[u], r, cc)

    def d_start(u):
        def one(d, carry):
            d_send(u, d).start()
            return carry

        lax.fori_loop(1, 16, one, 0)

    def d_rest(owner):
        @pl.when(r == owner)
        def _():
            for u in range(owner):
                dpart[u] = dot_nt(a_ref[0, 0:256, :], band[0, u]) + dot_nt(a_ref[1, 0:256, :], band[1, u])
                d_start(u)

    def piece_of(t, u):
        rows = pl.ds(pl.multiple_of(256 * t + 16 * c, 16), 16)
        return cm.at[rows, pl.ds(256 * u, 256)]

    def tile_of(t, u):
        return cm.at[pl.ds(pl.multiple_of(256 * t, 256), 256), pl.ds(256 * u, 256)]

    def rows_of(n):
        return cm.at[pl.ds(0, n), pl.ds(0, 256)]

    def sum_tiles(tt):
        for u in range(2 * tt + 2):

            @pl.when(jnp.logical_and(z == tt, u <= r))
            def _():
                wait_bytes(drs.at[u], d_r.at[u])
                total = dpart[u, pl.ds(pl.multiple_of(16 * c, 16), 16), :]
                for k in range(15):
                    total = total + drs[u, k]
                piece = piece_of(r, u)
                piece[...] = ebuf[0, :, 256 * u : 256 * u + 256] - total

                def one(d, carry):
                    remote(piece, piece, z_s.at[u], z_r.at[tt, u], 2 * ((z + d) % 8) + q, c).start()
                    return carry

                lax.fori_loop(1, 8, one, 0)

    def tiles(tt, fn):
        for u in range(2 * tt + 2):
            t = 2 * tt + q

            @pl.when(u <= t)
            def _():
                fn(tt, t, u)

    def gather(tt, t, u):
        piece = piece_of(t, u)

        @pl.when(r != t)
        def _():
            remote(piece, piece, z_s.at[u], z_r.at[tt, u], sib, c).wait_recv()

        def one(d, carry):
            remote(piece, piece, g_s.at[tt, u], g_r.at[tt, u], r, (c + d) % 16).start()
            return carry

        lax.fori_loop(1, 16, one, 0)

    def share(tt, t, u):
        wait_bytes(rows_of(240), g_r.at[tt, u])
        tile = tile_of(t, u)
        remote(tile, tile, gs_s.at[tt, u], gs_r.at[tt, u], sib, c).start()

    def shared(tt):
        for u in range(2 * tt + 2):
            t = 2 * tt + 1 - q

            @pl.when(u <= t)
            def _():
                wait_bytes(rows_of(256), gs_r.at[tt, u])

    def sent(tt):
        def one(tt, t, u):
            wait_bytes(rows_of(240), g_s.at[tt, u])
            wait_bytes(rows_of(256), gs_s.at[tt, u])

        tiles(tt, one)
        for u in range(2 * tt + 2):

            @pl.when(jnp.logical_and(z == tt, u <= r))
            def _():
                wait_bytes(drs.at[u], d_s.at[u])
                wait_bytes(rows_of(112), z_s.at[u])

    def product(i, carry):
        n, tl = i // 2, i % 2
        rows = pl.ds(pl.multiple_of(256 * tl, 256), 256)
        known = jnp.logical_and(r < 4, tl == 0)

        @pl.when(jnp.logical_and(known, n <= r))
        def _():
            for cc in range(16):
                part[slot(cc), n, 0:16, :] = dpart[n, 16 * cc : 16 * cc + 16, :]

        @pl.when(jnp.logical_and(known, n > r))
        def _():
            for cc in range(16):
                part[cc, n, 0:16, :] = jnp.zeros((16, 256), F32)

        @pl.when(jnp.logical_not(known))
        def _():
            res = dot_nt(a_ref[0, rows, :], band[0, n]) + dot_nt(a_ref[1, rows, :], band[1, n])
            for cc in range(16):
                part[slot(cc), n, pl.ds(pl.multiple_of(16 * tl, 16), 16), :] = res[16 * cc : 16 * cc + 16]

        return carry

    def products():
        lax.fori_loop(0, 8, product, 0)
        for d in (1, 2, 3):
            ff = (f + d) % 4
            remote(part.at[pl.ds(4 * ff, 4)], rs1.at[d - 1], r1_s, r1_r, r, col_of(ff, s)).start()

    def sum_first():
        wait_bytes(rs1, r1_r)

        def one(i, carry):
            k, n = i // 4, i % 4
            part[4 * f + k, n] = part[4 * f + k, n] + (rs1[0, k, n] + rs1[1, k, n] + rs1[2, k, n])
            return carry

        lax.fori_loop(0, 16, one, 0)
        for d in (1, 2, 3):
            sx = (s + d) % 4
            remote(part.at[4 * f + sx], rs2.at[d - 1], r2_s, r2_r, r, col_of(f, sx)).start()

    def sum_second():
        wait_bytes(rs2, r2_r)
        for n in range(4):
            total = part[4 * f + s, n] + (rs2[0, n] + rs2[1, n] + rs2[2, n])
            for tl in (0, 1):
                cm[1024 + 16 * tl : 1040 + 16 * tl, 256 * n : 256 * n + 256] = (
                    ebuf[tl, :, 256 * n : 256 * n + 256] - total[16 * tl : 16 * tl + 16]
                )

    def solve_rows(j):
        x = dot_nt(cm[1024:1056, BLK * j : BLK * j + BLK], winv[j])
        cm[1024:1056, BLK * j : BLK * j + BLK] = x
        if j < NB - 1:
            below = BLK * (j + 1)
            cm[1024:1056, below:1024] = cm[1024:1056, below:1024] - dot_nt(x, cm[below:1024, BLK * j : BLK * j + BLK])

    def blocks(first, last, bottom, rows_from, ticks, after):
        def block(j, carry):
            cols = pl.ds(pl.multiple_of(BLK * j, BLK), BLK)

            def read(i):
                return cm[pl.ds(pl.multiple_of(BLK * j + 8 * i, 8), 8), cols]

            def write(g, x):
                winv[j, 8 * g : 8 * g + 8, :] = x

            def poll(n):
                ring(ticks + 4 * j + n, ticks + 4 * j + n + 1)

            factor_inverse(read, write, poll if ticks else None)
            for n in range(first, last):

                @pl.when(j == n)
                def _():
                    if n == rows_from:
                        for k in range(n):
                            solve_rows(k)
                    top, end = BLK * (n + 1), (1056 if n >= rows_from else bottom)
                    if top < end:
                        x = dot_nt(cm[top:end, BLK * n : BLK * n + BLK], winv[n])
                        cm[top:end, BLK * n : BLK * n + BLK] = x
                        for kb in range(top, bottom, 256):
                            width = min(256, bottom - kb)
                            cm[kb:end, kb : kb + width] = cm[kb:end, kb : kb + width] - dot_nt(
                                x[kb - top :], x[kb - top : kb - top + width]
                            )
                    after(n)

            return carry

        lax.fori_loop(first, last, block, 0)

    @pl.when(r < 4)
    def _():
        d_start(r)

    ring(0, 4)

    @pl.when(z == 0)
    def _():
        from_sibling(0)

    d_rest(1)
    ring(4, 7)
    sum_tiles(0)
    ring(7, 10)
    tiles(0, gather)

    @pl.when(z == 1)
    def _():
        from_sibling(0)
        from_sibling(1)

    d_rest(2)
    d_rest(3)
    ring(10, 12)
    tiles(0, share)
    ring(12, 14)
    sum_tiles(1)
    shared(0)
    sent(0)

    def after_first(n):
        if n == 0:
            tiles(1, gather)
        if n == 2:
            ring_end()
            products()
            tiles(1, share)
        if n == 3:
            shared(1)
            sent(1)

    blocks(0, 4, 512, NB, 14, after_first)

    for k in range(4):
        x = dot_nt(cm[512:1024, BLK * k : BLK * k + BLK], winv[k])
        cm[512:1024, BLK * k : BLK * k + BLK] = x
        if k < 3:
            below = BLK * (k + 1)
            cm[512:1024, below:512] = cm[512:1024, below:512] - dot_nt(x, cm[below:512, BLK * k : BLK * k + BLK])
    for kb in (512, 768):
        cm[kb:1024, kb : kb + 256] = cm[kb:1024, kb : kb + 256] - dot_nt(cm[kb:1024, 0:512], cm[kb : kb + 256, 0:512])

    step = lax.broadcasted_iota(jnp.int32, (16, 64), 0)
    lanes = lax.broadcasted_iota(jnp.int32, (16, 64), 1)
    my_rows = pl.ds(pl.multiple_of(16 * c, 16), 16)

    def out_send(d):
        cc = (c + d) % 16
        return remote(stage.at[cc], outv.at[:, my_rows], o_s.at[d - 1], o_r.at[d - 1], r, cc)

    def out_start(first, last):
        for tl in (0, 1):
            g0 = (16 * tl + r) * 256 + 16 * c
            for cc in range(first, last):
                x = cm[1024 + 16 * tl : 1040 + 16 * tl, 64 * cc : 64 * cc + 64]
                stage[cc, tl] = jnp.where(lanes + 64 * cc <= step + g0, x, 0.0)

        def one(cc, carry):
            @pl.when(cc != c)
            def _():
                out_send((cc - c + 16) % 16).start()

            return carry

        lax.fori_loop(first, last, one, 0)

    def after_second(n):
        if n == 4:
            sum_first()
        if n == 5:
            sum_second()
        if n == 6:
            out_start(0, 14)

    blocks(4, 8, 1024, 6, 0, after_second)
    out_start(14, 16)
    outv[:, my_rows] = stage[c]

    wait_bytes(rs1, r1_s)
    wait_bytes(rs2, r2_s)

    def out_end(d, carry):
        copy = out_send(d)
        copy.wait_send()
        copy.wait_recv()
        return carry

    lax.fori_loop(1, 16, out_end, 0)
    for tl in (0, 1):
        out_ref[tl] = outv[tl].T


def per_device(old_factor, panel_block):
    a = jnp.transpose(old_factor, (2, 0, 1, 3)).reshape(2, 512, 256)
    dma = pltpu.SemaphoreType.DMA
    scratch = [
        pltpu.VMEM((2, 4, 256, 256), F32),
        pltpu.VMEM((16, 4, 32, 256), F32),
        pltpu.VMEM((3, 4, 4, 32, 256), F32),
        pltpu.VMEM((3, 4, 32, 256), F32),
        pltpu.VMEM((4, 256, 256), F32),
        pltpu.VMEM((4, 15, 16, 256), F32),
        pltpu.VMEM((1056, 1024), F32),
        pltpu.VMEM((NB, BLK, BLK), F32),
        pltpu.VMEM((16, 2, 16, 64), F32),
        pltpu.VMEM((2, 256, 64), F32),
        pltpu.VMEM((2, 16, 1024), F32),
        dma, dma((4 * NCH,)), dma((4 * NCH,)), dma((2 * NCH,)), dma((4 * NCH,)), dma((4 * NCH,)),
        dma((4,)), dma((4,)), dma((4,)), dma((2, 4)), dma((2, 4)), dma((2, 4)), dma((2, 4)), dma((2, 4)),
        dma, dma, dma, dma, dma((15,)), dma((15,)),
    ]
    out = pl.pallas_call(
        kernel,
        out_shape=jax.ShapeDtypeStruct((2, 64, 256), F32),
        in_specs=[pl.BlockSpec(memory_space=pltpu.VMEM), pl.BlockSpec(memory_space=pl.ANY)],
        out_specs=pl.BlockSpec(memory_space=pltpu.VMEM),
        scratch_shapes=scratch,
        compiler_params=pltpu.CompilerParams(
            collective_id=0, has_side_effects=True, vmem_limit_bytes=62 * 1024 * 1024
        ),
    )(a, panel_block)
    return jnp.transpose(out, (0, 2, 1))


def solution(mesh):
    return jax.shard_map(
        per_device,
        mesh=mesh,
        in_specs=(P(None, "row", None, "col"), P(None, "row", None)),
        out_specs=P(None, "row", "col"),
        check_vma=False,
    )
```

```python
import jax
import jax.numpy as jnp
from jax import lax
from jax.experimental import pallas as pl
from jax.experimental.pallas import tpu as pltpu
from jax.sharding import PartitionSpec as P

F32 = jnp.float32
MESH = pl.DeviceIdType.MESH
BLK = 128
NB = 8
SUPER = 2
NCH = 4
LAG = 3


def lane(x, k):
    return jnp.broadcast_to(x[:, k : k + 1], (8, BLK))


def sub(x, k):
    return jnp.broadcast_to(x[k : k + 1, :], (8, BLK))


def dot_tn(a, b):
    return lax.dot_general(
        a, b, (((0,), (0,)), ((), ())), precision=lax.Precision.HIGHEST, preferred_element_type=F32
    )


def dot_nt(a, b):
    return lax.dot_general(
        a, b, (((1,), (1,)), ((), ())), precision=lax.Precision.HIGHEST, preferred_element_type=F32
    )


def factor_inverse(read, write, poll=None):
    idx = lax.broadcasted_iota(jnp.int32, (8, BLK), 0)
    col = lax.broadcasted_iota(jnp.int32, (8, BLK), 1)
    groups = BLK // 8
    m = [read(i) for i in range(groups)]
    w = [jnp.where(col == idx + 8 * i, 1.0, 0.0).astype(F32) for i in range(groups)]
    u = [None] * groups
    uw = [None] * groups
    for g in range(groups):
        sb = g // SUPER
        near = list(range(g + 1, min(groups, SUPER * (sb + 2))))
        t, v = m[g], w[g]
        piv = ahead if g else [lane(t, 8 * g + k) for k in range(8)]
        ahead = [lane(m[g + 1], 8 * g + 8 + k) for k in range(8)] if g < groups - 1 else None
        low = {i: [lane(m[i], 8 * g + k) for k in range(8)] for i in near}
        rows, rows_w, mult = [], [], {i: [] for i in near}
        for k in range(8):
            scale = lax.rsqrt(sub(piv[k], k))
            mk = jnp.where(idx > k, piv[k] * scale, 0.0)
            rk, rwk = sub(t, k) * scale, sub(v, k) * scale
            rows.append(rk)
            rows_w.append(rwk)
            if k < 7:
                t, v = t - mk * rk, v - mk * rwk
            for i in near:
                mult[i].append(low[i][k] * scale)
            if ahead is not None:
                lk = mult[g + 1][k]
                ahead = [ahead[n] - lk * sub(lk, n) for n in range(8)]
            for n in range(k + 1, 8):
                q = sub(piv[n], k) * scale
                piv[n] = piv[n] - mk * q
                for i in near:
                    low[i][n] = low[i][n] - mult[i][k] * q
        ug, uwg = rows[0], rows_w[0]
        for k in range(1, 8):
            ug, uwg = jnp.where(idx == k, rows[k], ug), jnp.where(idx == k, rows_w[k], uwg)
        u[g], uw[g] = ug, uwg
        write(g, uwg)
        for i in near:
            a, b = m[i], w[i]
            for k in range(8):
                a, b = a - mult[i][k] * rows[k], b - mult[i][k] * rows_w[k]
            m[i], w[i] = a, b
        if poll is not None and g % 4 == 3:
            poll(g // 4)
        first = SUPER * (sb + 2)
        if g % SUPER == SUPER - 1 and first < groups:
            us = jnp.concatenate(u[SUPER * sb : g + 1], axis=0)
            ws = jnp.concatenate(uw[SUPER * sb : g + 1], axis=0)
            eu, ew = dot_tn(us, us), dot_tn(us, ws)
            for i in range(first, groups):
                m[i], w[i] = m[i] - eu[8 * i : 8 * i + 8], w[i] - ew[8 * i : 8 * i + 8]


def kernel(
    a_ref, e_hbm, out_ref,
    band, part, rs1, rs2, dpart, drs, cm, winv, stage, outv, ebuf,
    e_sem, ring_s, ring_r, back_s, sib_s, sib_r,
    d_s, d_r, z_s, z_r, g_s, g_r, gs_s, gs_r,
    r1_s, r1_r, r2_s, r2_r, o_s, o_r,
):
    r, c = lax.axis_index("row"), lax.axis_index("col")
    z, q = r // 2, r % 2
    sib = r + 1 - 2 * q
    sf, ss = 1 + 3 * q, 4 - 3 * q
    f, s = (c // sf) % 4, (c // ss) % 4

    def slot(cc):
        return 4 * ((cc // sf) % 4) + (cc // ss) % 4

    def col_of(ff, sx):
        return ff * sf + sx * ss

    def remote(src, dst, send, recv, row, colm):
        return pltpu.make_async_remote_copy(
            src_ref=src, dst_ref=dst, send_sem=send, recv_sem=recv, device_id=(row, colm), device_id_type=MESH
        )

    def wait_bytes(ref, sem):
        pltpu.make_async_copy(ref, ref, sem).wait()

    e_copy = pltpu.make_async_copy(e_hbm.at[:, pl.ds(pl.multiple_of(16 * c, 16), 16), :], ebuf, e_sem)
    e_copy.start()

    barrier = pltpu.get_barrier_semaphore()

    def greet(d, carry):
        pl.semaphore_signal(barrier, inc=1, device_id=(r, (c + d) % 16), device_id_type=MESH)
        return carry

    pl.semaphore_signal(barrier, inc=1, device_id=(sib, c), device_id_type=MESH)
    for d in range(1, 8):
        pl.semaphore_signal(barrier, inc=1, device_id=(2 * ((z + d) % 8) + q, c), device_id_type=MESH)
    lax.fori_loop(1, 16, greet, 0)

    @pl.when(r < 4)
    def _():
        low, high = a_ref[0, 0:256, :], a_ref[1, 0:256, :]
        band[0, r] = low
        band[1, r] = high
        dpart[r] = dot_nt(low, low) + dot_nt(high, high)

    e_copy.wait()
    pl.semaphore_wait(barrier, 23)

    def chain(h, i):
        pos = z if h == 0 else (9 - z) % 8
        nxt, prv = ((z + 1) % 8, (z + 7) % 8) if h == 0 else ((z + 7) % 8, (z + 1) % 8)
        is_a = (i // NCH + jnp.where(pos == 0, 1, 0)) % 2
        tile = (q + 2 - 2 * is_a) if h == 0 else (q + 2 * is_a)
        k = i % NCH
        n = 2 * NCH * h + NCH * is_a + k
        mine = band.at[h, tile, pl.ds(pl.multiple_of(256 // NCH * k, 256 // NCH), 256 // NCH)]
        fwd = remote(mine, mine, ring_s.at[n], ring_r.at[n], 2 * nxt + q, c)
        back = remote(mine, mine, back_s.at[NCH * h + k], ring_r.at[n], 2 * prv + q, c)
        to_sib = remote(mine, mine, sib_s.at[n], sib_r.at[n], sib, c)
        origin = pos == 1 - is_a
        forwards = jnp.logical_and(pos < 7, pos + is_a > 0)
        returns = jnp.logical_and(pos == 1, is_a == 0)
        return fwd, back, to_sib, origin, forwards, returns

    def ring_step(tick, carry):
        for h in (0, 1):
            pos = z if h == 0 else (9 - z) % 8
            late_by = LAG * jnp.maximum(pos - 1, 0)
            i = jnp.clip(tick - late_by, 0, 2 * NCH - 1)

            @pl.when(jnp.logical_and(tick >= late_by, tick < late_by + 2 * NCH))
            def _():
                fwd, back, to_sib, origin, forwards, returns = chain(h, i)

                @pl.when(jnp.logical_not(origin))
                def _():
                    fwd.wait_recv()

                @pl.when(forwards)
                def _():
                    fwd.start()

                @pl.when(returns)
                def _():
                    back.start()

                to_sib.start()

        return carry

    def ring(first, last):
        lax.fori_loop(first, last, ring_step, 0)

    def from_sibling(second):
        def one(k, carry):
            for h in (0, 1):
                is_a = 1 - second if h == 0 else second
                n = 2 * NCH * h + NCH * is_a + k
                theirs = band.at[h, 1 - q + 2 * second, pl.ds(pl.multiple_of(256 // NCH * k, 256 // NCH), 256 // NCH)]
                remote(theirs, theirs, sib_s.at[n], sib_r.at[n], sib, c).wait_recv()
            return carry

        lax.fori_loop(0, NCH, one, 0)

    def ring_end():
        def one(i, carry):
            for h in (0, 1):
                fwd, back, to_sib, origin, forwards, returns = chain(h, i)

                @pl.when(forwards)
                def _():
                    fwd.wait_send()

                @pl.when(returns)
                def _():
                    back.wait_send()

                to_sib.wait_send()
            return carry

        lax.fori_loop(0, 2 * NCH, one, 0)

        @pl.when(z > 1)
        def _():
            from_sibling(0)

        @pl.when(z != 1)
        def _():
            from_sibling(1)

    def d_send(u, d):
        cc = (c + d) % 16
        rows = pl.ds(pl.multiple_of(16 * cc, 16), 16)
        return remote(dpart.at[u, rows], drs.at[u, d - 1], d_s.at[u], d_r.at[u], r, cc)

    def d_start(u):
        def one(d, carry):
            d_send(u, d).start()
            return carry

        lax.fori_loop(1, 16, one, 0)

    def d_rest(owner):
        @pl.when(r == owner)
        def _():
            for u in range(owner):
                dpart[u] = dot_nt(a_ref[0, 0:256, :], band[0, u]) + dot_nt(a_ref[1, 0:256, :], band[1, u])
                d_start(u)

    def piece_of(t, u):
        rows = pl.ds(pl.multiple_of(256 * t + 16 * c, 16), 16)
        return cm.at[rows, pl.ds(256 * u, 256)]

    def tile_of(t, u):
        return cm.at[pl.ds(pl.multiple_of(256 * t, 256), 256), pl.ds(256 * u, 256)]

    def rows_of(n):
        return cm.at[pl.ds(0, n), pl.ds(0, 256)]

    def sum_tiles(tt):
        for u in range(2 * tt + 2):

            @pl.when(jnp.logical_and(z == tt, u <= r))
            def _():
                wait_bytes(drs.at[u], d_r.at[u])
                total = dpart[u, pl.ds(pl.multiple_of(16 * c, 16), 16), :]
                for k in range(15):
                    total = total + drs[u, k]
                piece = piece_of(r, u)
                piece[...] = ebuf[0, :, 256 * u : 256 * u + 256] - total

                def one(d, carry):
                    remote(piece, piece, z_s.at[u], z_r.at[tt, u], 2 * ((z + d) % 8) + q, c).start()
                    return carry

                lax.fori_loop(1, 8, one, 0)

    def tiles(tt, fn):
        for u in range(2 * tt + 2):
            t = 2 * tt + q

            @pl.when(u <= t)
            def _():
                fn(tt, t, u)

    def gather(tt, t, u):
        piece = piece_of(t, u)

        @pl.when(r != t)
        def _():
            remote(piece, piece, z_s.at[u], z_r.at[tt, u], sib, c).wait_recv()

        def one(d, carry):
            remote(piece, piece, g_s.at[tt, u], g_r.at[tt, u], r, (c + d) % 16).start()
            return carry

        lax.fori_loop(1, 16, one, 0)

    def share(tt, t, u):
        wait_bytes(rows_of(240), g_r.at[tt, u])
        tile = tile_of(t, u)
        remote(tile, tile, gs_s.at[tt, u], gs_r.at[tt, u], sib, c).start()

    def shared(tt):
        for u in range(2 * tt + 2):
            t = 2 * tt + 1 - q

            @pl.when(u <= t)
            def _():
                wait_bytes(rows_of(256), gs_r.at[tt, u])

    def sent(tt):
        def one(tt, t, u):
            wait_bytes(rows_of(240), g_s.at[tt, u])
            wait_bytes(rows_of(256), gs_s.at[tt, u])

        tiles(tt, one)
        for u in range(2 * tt + 2):

            @pl.when(jnp.logical_and(z == tt, u <= r))
            def _():
                wait_bytes(drs.at[u], d_s.at[u])
                wait_bytes(rows_of(112), z_s.at[u])

    def product(i, carry):
        n, tl = i // 2, i % 2
        rows = pl.ds(pl.multiple_of(256 * tl, 256), 256)
        known = jnp.logical_and(r < 4, tl == 0)

        @pl.when(jnp.logical_and(known, n <= r))
        def _():
            for cc in range(16):
                part[slot(cc), n, 0:16, :] = dpart[n, 16 * cc : 16 * cc + 16, :]

        @pl.when(jnp.logical_and(known, n > r))
        def _():
            for cc in range(16):
                part[cc, n, 0:16, :] = jnp.zeros((16, 256), F32)

        @pl.when(jnp.logical_not(known))
        def _():
            res = dot_nt(a_ref[0, rows, :], band[0, n]) + dot_nt(a_ref[1, rows, :], band[1, n])
            for cc in range(16):
                part[slot(cc), n, pl.ds(pl.multiple_of(16 * tl, 16), 16), :] = res[16 * cc : 16 * cc + 16]

        return carry

    def products():
        lax.fori_loop(0, 8, product, 0)
        for d in (1, 2, 3):
            ff = (f + d) % 4
            remote(part.at[pl.ds(4 * ff, 4)], rs1.at[d - 1], r1_s, r1_r, r, col_of(ff, s)).start()

    def sum_first():
        wait_bytes(rs1, r1_r)

        def one(i, carry):
            k, n = i // 4, i % 4
            part[4 * f + k, n] = part[4 * f + k, n] + (rs1[0, k, n] + rs1[1, k, n] + rs1[2, k, n])
            return carry

        lax.fori_loop(0, 16, one, 0)
        for d in (1, 2, 3):
            sx = (s + d) % 4
            remote(part.at[4 * f + sx], rs2.at[d - 1], r2_s, r2_r, r, col_of(f, sx)).start()

    def sum_second():
        wait_bytes(rs2, r2_r)
        for n in range(4):
            total = part[4 * f + s, n] + (rs2[0, n] + rs2[1, n] + rs2[2, n])
            for tl in (0, 1):
                cm[1024 + 16 * tl : 1040 + 16 * tl, 256 * n : 256 * n + 256] = (
                    ebuf[tl, :, 256 * n : 256 * n + 256] - total[16 * tl : 16 * tl + 16]
                )

    def solve_rows(j):
        x = dot_nt(cm[1024:1056, BLK * j : BLK * j + BLK], winv[j])
        cm[1024:1056, BLK * j : BLK * j + BLK] = x
        if j < NB - 1:
            below = BLK * (j + 1)
            cm[1024:1056, below:1024] = cm[1024:1056, below:1024] - dot_nt(x, cm[below:1024, BLK * j : BLK * j + BLK])

    def blocks(first, last, bottom, rows_from, ticks, after):
        def block(j, carry):
            cols = pl.ds(pl.multiple_of(BLK * j, BLK), BLK)

            def read(i):
                return cm[pl.ds(pl.multiple_of(BLK * j + 8 * i, 8), 8), cols]

            def write(g, x):
                winv[j, 8 * g : 8 * g + 8, :] = x

            def poll(n):
                ring(ticks + 4 * j + n, ticks + 4 * j + n + 1)

            factor_inverse(read, write, poll if ticks else None)
            for n in range(first, last):

                @pl.when(j == n)
                def _():
                    if n == rows_from:
                        for k in range(n):
                            solve_rows(k)
                    top, end = BLK * (n + 1), (1056 if n >= rows_from else bottom)
                    if top < end:
                        x = dot_nt(cm[top:end, BLK * n : BLK * n + BLK], winv[n])
                        cm[top:end, BLK * n : BLK * n + BLK] = x
                        for kb in range(top, bottom, 256):
                            width = min(256, bottom - kb)
                            cm[kb:end, kb : kb + width] = cm[kb:end, kb : kb + width] - dot_nt(
                                x[kb - top :], x[kb - top : kb - top + width]
                            )
                    after(n)

            return carry

        lax.fori_loop(first, last, block, 0)

    @pl.when(r < 4)
    def _():
        d_start(r)

    ring(0, 4)

    @pl.when(z == 0)
    def _():
        from_sibling(0)

    d_rest(1)
    ring(4, 7)
    sum_tiles(0)
    ring(7, 10)
    tiles(0, gather)

    @pl.when(z == 1)
    def _():
        from_sibling(0)
        from_sibling(1)

    d_rest(2)
    d_rest(3)
    ring(10, 12)
    tiles(0, share)
    ring(12, 14)
    shared(0)
    sent(0)

    def after_first(n):
        if n == 0:
            sum_tiles(1)
        if n == 1:
            tiles(1, gather)
        if n == 2:
            ring_end()
            products()
            tiles(1, share)
        if n == 3:
            shared(1)
            sent(1)

    blocks(0, 4, 512, NB, 14, after_first)

    for k in range(4):
        x = dot_nt(cm[512:1024, BLK * k : BLK * k + BLK], winv[k])
        cm[512:1024, BLK * k : BLK * k + BLK] = x
        if k < 3:
            below = BLK * (k + 1)
            cm[512:1024, below:512] = cm[512:1024, below:512] - dot_nt(x, cm[below:512, BLK * k : BLK * k + BLK])
    for kb in (512, 768):
        cm[kb:1024, kb : kb + 256] = cm[kb:1024, kb : kb + 256] - dot_nt(cm[kb:1024, 0:512], cm[kb : kb + 256, 0:512])

    step = lax.broadcasted_iota(jnp.int32, (16, 64), 0)
    lanes = lax.broadcasted_iota(jnp.int32, (16, 64), 1)
    my_rows = pl.ds(pl.multiple_of(16 * c, 16), 16)

    def out_send(d):
        cc = (c + d) % 16
        return remote(stage.at[cc], outv.at[:, my_rows], o_s.at[d - 1], o_r.at[d - 1], r, cc)

    def out_start(first, last):
        for tl in (0, 1):
            g0 = (16 * tl + r) * 256 + 16 * c
            for cc in range(first, last):
                x = cm[1024 + 16 * tl : 1040 + 16 * tl, 64 * cc : 64 * cc + 64]
                stage[cc, tl] = jnp.where(lanes + 64 * cc <= step + g0, x, 0.0)

        def one(cc, carry):
            @pl.when(cc != c)
            def _():
                out_send((cc - c + 16) % 16).start()

            return carry

        lax.fori_loop(first, last, one, 0)

    def after_second(n):
        if n == 4:
            sum_first()
        if n == 5:
            sum_second()
        if n == 6:
            out_start(0, 14)

    blocks(4, 8, 1024, 6, 0, after_second)
    out_start(14, 16)
    outv[:, my_rows] = stage[c]

    wait_bytes(rs1, r1_s)
    wait_bytes(rs2, r2_s)

    def out_end(d, carry):
        copy = out_send(d)
        copy.wait_send()
        copy.wait_recv()
        return carry

    lax.fori_loop(1, 16, out_end, 0)
    for tl in (0, 1):
        out_ref[tl] = outv[tl].T


def per_device(old_factor, panel_block):
    a = jnp.transpose(old_factor, (2, 0, 1, 3)).reshape(2, 512, 256)
    dma = pltpu.SemaphoreType.DMA
    scratch = [
        pltpu.VMEM((2, 4, 256, 256), F32),
        pltpu.VMEM((16, 4, 32, 256), F32),
        pltpu.VMEM((3, 4, 4, 32, 256), F32),
        pltpu.VMEM((3, 4, 32, 256), F32),
        pltpu.VMEM((4, 256, 256), F32),
        pltpu.VMEM((4, 15, 16, 256), F32),
        pltpu.VMEM((1056, 1024), F32),
        pltpu.VMEM((NB, BLK, BLK), F32),
        pltpu.VMEM((16, 2, 16, 64), F32),
        pltpu.VMEM((2, 256, 64), F32),
        pltpu.VMEM((2, 16, 1024), F32),
        dma, dma((4 * NCH,)), dma((4 * NCH,)), dma((2 * NCH,)), dma((4 * NCH,)), dma((4 * NCH,)),
        dma((4,)), dma((4,)), dma((4,)), dma((2, 4)), dma((2, 4)), dma((2, 4)), dma((2, 4)), dma((2, 4)),
        dma, dma, dma, dma, dma((15,)), dma((15,)),
    ]
    out = pl.pallas_call(
        kernel,
        out_shape=jax.ShapeDtypeStruct((2, 64, 256), F32),
        in_specs=[pl.BlockSpec(memory_space=pltpu.VMEM), pl.BlockSpec(memory_space=pl.ANY)],
        out_specs=pl.BlockSpec(memory_space=pltpu.VMEM),
        scratch_shapes=scratch,
        compiler_params=pltpu.CompilerParams(
            collective_id=0, has_side_effects=True, vmem_limit_bytes=62 * 1024 * 1024
        ),
    )(a, panel_block)
    return jnp.transpose(out, (0, 2, 1))


def solution(mesh):
    return jax.shard_map(
        per_device,
        mesh=mesh,
        in_specs=(P(None, "row", None, "col"), P(None, "row", None)),
        out_specs=P(None, "row", "col"),
        check_vma=False,
    )
```
